256 devices in a mesh: grp: 32 (over y, z), sp: 8 (over x, core).
Axes of the slice: x: 4, y: 4, z: 8, core: 2. Of those that a mesh axis runs over, the one named last changes fastest.
Arguments:
- queries: bfloat16 [32768, 4096], P(('grp', 'sp')), may hold values from -5 to 5
- key_row_matrix: bfloat16 [32768, 1024], P(('grp', 'sp')), may hold values from -5 to 5
- value_row_matrix: bfloat16 [32768, 1024], P(('grp', 'sp')), may hold values from -6 to 6
- out_grad: bfloat16 [32768, 4096], P(('grp', 'sp')), may hold values from -6 to 6
- dest_group: int32 [32, 1024], P('grp', 'sp'), may hold values from 0 to 31, as said below
- source_group: int32 [32, 1024], P('grp', 'sp'), may hold values from 0 to 31, as said below
- seq_start: int32 [32, 1024], P('grp'), may hold values from 0 to 768, as said below
Outputs:
- attended: bfloat16 [32768, 4096], P(('grp', 'sp'))
- query_grad: bfloat16 [32768, 4096], P(('grp', 'sp'))
- key_gradient: bfloat16 [32768, 1024], P(('grp', 'sp'))
- value_gradient: bfloat16 [32768, 1024], P(('grp', 'sp'))
The draws below stay inside these ranges and needn't reach their ends.
Inputs may be any that keep to these rules, and one draw needn't show every extreme that they name: `dest_group`: for each index s of sp and groups g, g2, the tokens of device (g, s) sent to g2 are as many as the positions of column s of group g2 whose source is g; this count is even, at most 8, and equals 8 for some pair in every column. Entries come in equal aligned pairs (i even, i + 1). `source_group`: the counterpart of dest_group: entries come in equal aligned pairs, and each group source count matches dest_group as stated there. `seq_start`: Even, at most the position itself, equal for all positions of one sequence and rising only where a sequence begins; a group holds one or two sequences.
All inputs are finite; a program needn't handle non-finite values.
Results may differ from the reference program's by a relative error of at most 0.0072.
Values may be sent and summed in bfloat16 or wider, within the bound.
No kernel may reach another device: no remote copies, remote signals or barrier semaphores. Data moves between devices by JAX's collectives and lax.ppermute only.
A program may use at most 128 MiB of HBM per device.

```python
import math
import jax
import jax.numpy as jnp
from jax import lax

HQ = 32
KEY_VALUE_HEADS = 8
HEAD_SIZE = 128
TOK_DEV = 128
TOTAL_TOKENS = 32768
GROUP_ROWS = 1024
CAP = 8
N_GRP = 32
N_SP = 8


def routing_tables(key):
    half_mean = TOK_DEV // (2 * N_GRP)
    pair_slots = TOK_DEV // 2

    def labels(pair_counts, label_key):
        bounds = jnp.cumsum(pair_counts)
        places = jnp.arange(pair_slots)
        sorted_labels = jnp.sum((places[:, None] >= bounds[None, :]).astype(jnp.int32), axis=1)
        shuffle = jax.random.permutation(label_key, pair_slots)
        return jnp.repeat(sorted_labels[shuffle], 2)

    def column(column_key):
        raises = jax.random.randint(jax.random.fold_in(column_key, 1), (N_GRP,), 0, half_mean + 1)
        raises = raises.at[0].set(half_mean).at[1].set(0)
        widths = half_mean + raises - jnp.roll(raises, -1)
        col_perm = jax.random.permutation(jax.random.fold_in(column_key, 2), N_GRP)
        row_perm = jax.random.permutation(jax.random.fold_in(column_key, 3), N_GRP)
        counts = widths[(col_perm[None, :] - row_perm[:, None]) % N_GRP]
        send_keys = jax.random.split(jax.random.fold_in(column_key, 4), N_GRP)
        recv_keys = jax.random.split(jax.random.fold_in(column_key, 5), N_GRP)
        send_rows = jax.vmap(labels)(counts, send_keys)
        recv_rows = jax.vmap(labels)(counts.T, recv_keys)
        return (send_rows, recv_rows)
    column_keys = jax.vmap(lambda column_index: jax.random.fold_in(key, column_index))(jnp.arange(N_SP))
    send_all, recv_all = jax.vmap(column)(column_keys)
    send_all = jnp.transpose(send_all, (1, 0, 2)).reshape(N_GRP, N_SP * TOK_DEV)
    recv_all = jnp.transpose(recv_all, (1, 0, 2)).reshape(N_GRP, N_SP * TOK_DEV)
    return (send_all.astype(jnp.int32), recv_all.astype(jnp.int32))


def draw_queries(key, part):
    key = jax.random.fold_in(key, 7)
    return jnp.clip(jax.random.normal(key, (TOTAL_TOKENS, HQ * HEAD_SIZE)), -4.5, 4.5).astype(jnp.bfloat16)


def draw_key_row_matrix(key, part):
    key = jax.random.fold_in(key, 8)
    return jnp.clip(jax.random.normal(key, (TOTAL_TOKENS, KEY_VALUE_HEADS * HEAD_SIZE)), -4.5, 4.5).astype(jnp.bfloat16)


def draw_dest_group(key, part):
    return routing_tables(key)[0]


def draw_source_group(key, part):
    return routing_tables(key)[1]


def draw_seq_start(key, part):
    key = jax.random.fold_in(key, 5)
    cut_points = 2 * jax.random.randint(jax.random.fold_in(key, 1), (N_GRP,), GROUP_ROWS // 8, 3 * GROUP_ROWS // 8 + 1)
    active = jax.random.randint(jax.random.fold_in(key, 2), (N_GRP,), 0, 2)
    cut_points = cut_points * active
    cut_points = cut_points.at[0].set(3 * GROUP_ROWS // 4)
    places = jnp.arange(GROUP_ROWS)
    picked = jnp.where(cut_points[:, None] <= places[None, :], cut_points[:, None], 0)
    return picked.astype(jnp.int32)


def block_levels(own_key, dims, pieces, least, high):
    def one(dim, shards_of):
        draws = jax.random.uniform(jax.random.fold_in(jax.random.fold_in(own_key, 6), dim), (shards_of,), jnp.float32, least / len(pieces), high / len(pieces))
        return jnp.repeat(jnp.exp(draws), dims[dim] // shards_of).reshape((-1,) + (1,) * (len(dims) - dim - 1))

    factor_of = one(*pieces[0])
    for cut in pieces[1:]:
        factor_of = factor_of * one(*cut)
    return factor_of


def normal_values(rng, dims, width, most, shards=(), kind=jnp.bfloat16):
    values = width * jax.random.normal(rng, dims, jnp.float32)
    if shards:
        values = values * block_levels(rng, dims, shards, -0.22, 0.18)
    return jnp.clip(values, -most, most).astype(kind)


def setup_inputs(seed: int = 0) -> dict:
    arg_keys = jax.random.split(jax.random.key(seed), 8)
    queries = draw_queries(jax.random.fold_in(arg_keys[7], 71), 0)
    key_row_matrix = draw_key_row_matrix(jax.random.fold_in(arg_keys[7], 71), 0)
    value_row_matrix = normal_values(arg_keys[2], (TOTAL_TOKENS, KEY_VALUE_HEADS * HEAD_SIZE), 1.0, 6.0, ((0, 256),))
    out_grad = normal_values(arg_keys[3], (TOTAL_TOKENS, HQ * HEAD_SIZE), 1.0, 6.0, ((0, 256),))
    dest_group = draw_dest_group(jax.random.fold_in(arg_keys[7], 71), 0)
    source_group = draw_source_group(jax.random.fold_in(arg_keys[7], 71), 0)
    seq_start = draw_seq_start(jax.random.fold_in(arg_keys[7], 71), 0)
    return dict(queries=queries, key_row_matrix=key_row_matrix, value_row_matrix=value_row_matrix, out_grad=out_grad, dest_group=dest_group, source_group=source_group, seq_start=seq_start)


def rank_within(labels, count):
    marks = (labels[:, None] == jnp.arange(count, dtype=jnp.int32)[None, :]).astype(jnp.int32)
    before = (jnp.cumsum(marks, axis=0) - marks).astype(jnp.int32)
    return lax.optimization_barrier(jnp.sum(before * marks, axis=1)).astype(jnp.int32)

def home_rows(dest_group, source_group):
    dest_table = dest_group.reshape(N_GRP, N_SP, TOK_DEV)
    source_table = source_group.reshape(N_GRP, N_SP, TOK_DEV)
    ranker = jax.vmap(jax.vmap(lambda labels: rank_within(labels, N_GRP)))
    send_rank = ranker(dest_table)
    recv_rank = ranker(source_table)
    group_index = jnp.arange(N_GRP, dtype=jnp.int32)[:, None, None]
    column_index = jnp.arange(N_SP, dtype=jnp.int32)[None, :, None]
    row_index = jnp.arange(TOK_DEV, dtype=jnp.int32)[None, None, :]
    token_index = ((group_index * N_SP + column_index) * TOK_DEV + row_index).astype(jnp.int32)
    token_index = jnp.broadcast_to(token_index, (N_GRP, N_SP, TOK_DEV))
    table = jnp.zeros((N_GRP, N_SP, N_GRP, CAP), jnp.int32)
    table = table.at[jnp.broadcast_to(group_index, dest_table.shape), jnp.broadcast_to(column_index, dest_table.shape), dest_table, send_rank].set(token_index)
    found = table[source_table, jnp.broadcast_to(column_index, source_table.shape), jnp.broadcast_to(group_index, source_table.shape), recv_rank]
    return found.reshape(N_GRP, N_SP * TOK_DEV).astype(jnp.int32)

def head_block(query_part, grad_part, positions, starts, key_part, value_part, scaling):
    key_place = jnp.arange(key_part.shape[0], dtype=jnp.int32)
    visible = (key_place[None, :] >= starts[:, None]) & (key_place[None, :] <= positions[:, None])
    scores = jnp.dot(query_part, key_part.T, preferred_element_type=jnp.float32) * scaling
    scores = jnp.where(visible, scores, -jnp.inf)
    powers = jnp.exp(scores - lax.optimization_barrier(jnp.max(scores, axis=1, keepdims=True)))
    probability = powers / lax.optimization_barrier(jnp.sum(powers, axis=1, keepdims=True))
    weights = probability.astype(jnp.bfloat16)
    output = jnp.dot(weights, value_part, preferred_element_type=jnp.float32).astype(jnp.bfloat16)
    prob_grad = jnp.dot(grad_part, value_part.T, preferred_element_type=jnp.float32)
    spread = lax.optimization_barrier(jnp.sum(probability * prob_grad, axis=1, keepdims=True))
    dscore = (probability * (prob_grad - spread) * scaling).astype(jnp.bfloat16)
    grad_query = jnp.dot(dscore, key_part, preferred_element_type=jnp.float32).astype(jnp.bfloat16)
    key_gradient_fn = jnp.dot(dscore.T, query_part, preferred_element_type=jnp.float32)
    value_gradient_fn = jnp.dot(weights.T, grad_part, preferred_element_type=jnp.float32)
    return (output, grad_query, key_gradient_fn, value_gradient_fn)

def attend(query_rows, key_all, value_all, grad_rows, positions, starts):
    query_count = query_rows.shape[0]
    kv_heads = key_all.shape[1] // HEAD_SIZE
    group_share = query_rows.shape[1] // key_all.shape[1]
    flat_rows = query_count * group_share
    block_rows = 512 if flat_rows % 512 == 0 else flat_rows
    scaling = 1.0 / math.sqrt(HEAD_SIZE)
    head_width = group_share * HEAD_SIZE
    pos_rows = jnp.broadcast_to(positions[:, None], (query_count, group_share)).reshape(flat_rows)
    start_rows = jnp.broadcast_to(starts[:, None], (query_count, group_share)).reshape(flat_rows)
    outputs, query_grads, key_grads, value_grads = ([], [], [], [])
    for head_index in range(kv_heads):
        query_head = query_rows[:, head_index * head_width:(head_index + 1) * head_width].reshape(flat_rows, HEAD_SIZE)
        grad_head = grad_rows[:, head_index * head_width:(head_index + 1) * head_width].reshape(flat_rows, HEAD_SIZE)
        key_head = key_all[:, head_index * HEAD_SIZE:(head_index + 1) * HEAD_SIZE]
        value_head = value_all[:, head_index * HEAD_SIZE:(head_index + 1) * HEAD_SIZE]

        def advance(carry, block_index):
            first = block_index * block_rows
            result = head_block(lax.dynamic_slice_in_dim(query_head, first, block_rows, 0), lax.dynamic_slice_in_dim(grad_head, first, block_rows, 0), lax.dynamic_slice_in_dim(pos_rows, first, block_rows, 0), lax.dynamic_slice_in_dim(start_rows, first, block_rows, 0), key_head, value_head, scaling)
            return ((carry[0] + result[2], carry[1] + result[3]), (result[0], result[1]))
        zero_rows = jnp.zeros((key_all.shape[0], HEAD_SIZE), jnp.float32)
        sums, stacked = lax.scan(advance, (zero_rows, zero_rows), jnp.arange(flat_rows // block_rows, dtype=jnp.int32))
        outputs.append(stacked[0].reshape(query_count, head_width))
        query_grads.append(stacked[1].reshape(query_count, head_width))
        key_grads.append(sums[0])
        value_grads.append(sums[1])
    return (jnp.concatenate(outputs, axis=1), jnp.concatenate(query_grads, axis=1), jnp.concatenate(key_grads, axis=1), jnp.concatenate(value_grads, axis=1))

def reference(queries, key_row_matrix, value_row_matrix, out_grad, dest_group, source_group, seq_start):
    home = home_rows(dest_group, source_group)
    positions = jnp.arange(GROUP_ROWS, dtype=jnp.int32)

    def one_group(packed):
        tokens, starts = packed
        result = attend(queries[tokens], key_row_matrix[tokens], value_row_matrix[tokens], out_grad[tokens], positions, starts)
        return (result[0], result[1], result[2].astype(jnp.bfloat16), result[3].astype(jnp.bfloat16))
    output, grad_query, key_gradient_fn, value_gradient_fn = lax.map(one_group, (home, seq_start))
    flattened_home = home.reshape(-1)
    attended = jnp.zeros(queries.shape, queries.dtype).at[flattened_home].set(output.reshape(-1, HQ * HEAD_SIZE))
    query_grad = jnp.zeros(queries.shape, queries.dtype).at[flattened_home].set(grad_query.reshape(-1, HQ * HEAD_SIZE))
    key_gradient = jnp.zeros(key_row_matrix.shape, key_row_matrix.dtype).at[flattened_home].set(key_gradient_fn.reshape(-1, KEY_VALUE_HEADS * HEAD_SIZE))
    value_gradient = jnp.zeros(value_row_matrix.shape, value_row_matrix.dtype).at[flattened_home].set(value_gradient_fn.reshape(-1, KEY_VALUE_HEADS * HEAD_SIZE))
    return (attended, query_grad, key_gradient, value_gradient)
```

```python
import math

import jax
import jax.numpy as jnp
from jax import lax
from jax.experimental import pallas as pl
from jax.experimental.pallas import tpu as pltpu
from jax.sharding import PartitionSpec as P

HEAD = 128
F32 = jnp.float32
BF16 = jnp.bfloat16
VMEM_BYTES = 56 * 1024 * 1024


def slot_tables(labels, capacity):
    count = labels.shape[1]
    across = jnp.broadcast_to(labels.astype(F32), (count, count))
    down = across.T
    i = lax.broadcasted_iota(jnp.int32, (count, count), 0)
    j = lax.broadcasted_iota(jnp.int32, (count, count), 1)
    same = across == down
    rank_row = jnp.sum(jnp.where(same & (i < j), 1.0, 0.0), axis=0, keepdims=True)
    rank_col = jnp.sum(jnp.where(same & (j < i), 1.0, 0.0), axis=1, keepdims=True)
    slot_row = across[:1, :] * capacity + rank_row
    slot_col = down[:, :1] * capacity + rank_col
    return slot_row.astype(jnp.int32), slot_col.astype(jnp.int32)


def one_hot_rows(slot_row, total):
    t = lax.broadcasted_iota(jnp.int32, (total, slot_row.shape[1]), 0)
    return jnp.where(t == slot_row, 1.0, 0.0).astype(BF16)


def one_hot_cols(slot_col, total):
    t = lax.broadcasted_iota(jnp.int32, (slot_col.shape[0], total), 1)
    return jnp.where(t == slot_col, 1.0, 0.0).astype(BF16)


def pick(marks, rows):
    return jnp.dot(marks, rows, preferred_element_type=F32).astype(BF16)


def pack_kernel(capacity, labels_ref, q_ref, g_ref, k_ref, v_ref, out_ref, marks_ref):
    total = out_ref.shape[1]

    @pl.when(pl.program_id(0) == 0)
    def _():
        slot_row, _ = slot_tables(labels_ref[...], capacity)
        marks_ref[...] = one_hot_rows(slot_row, total)

    rows = jnp.concatenate([q_ref[...], g_ref[...], k_ref[...], v_ref[...]], axis=1)
    out_ref[0] = pick(marks_ref[...], rows)


def unpack_kernel(capacity, labels_ref, got_ref, o_ref, dq_ref, dk_ref, dv_ref, marks_ref):
    total = got_ref.shape[1]
    wide = o_ref.shape[1]

    @pl.when(pl.program_id(0) == 0)
    def _():
        _, slot_col = slot_tables(labels_ref[...], capacity)
        marks_ref[...] = one_hot_cols(slot_col, total)

    rows = pick(marks_ref[...], got_ref[0])
    o_ref[...] = rows[:, :wide]
    dq_ref[...] = rows[:, wide : 2 * wide]
    dk_ref[...] = rows[:, 2 * wide : 2 * wide + HEAD]
    dv_ref[...] = rows[:, 2 * wide + HEAD :]


def attend_kernel(
    capacity, got_ref, source_ref, start_ref, out_ref, x_ref, y_ref, kt_ref, vt_ref, dk_ref, dv_ref
):
    columns, total, width = got_ref.shape
    tok = source_ref.shape[1]
    share = (width - 2 * HEAD) // (2 * HEAD)
    wide = share * HEAD
    scaling = 1.0 / math.sqrt(HEAD)
    power_scale = scaling * math.log2(math.e)
    across = (((1,), (1,)), ((), ()))
    k_cols = slice(2 * wide, 2 * wide + HEAD)
    v_cols = slice(2 * wide + HEAD, 2 * wide + 2 * HEAD)
    slots = [slot_tables(source_ref[s : s + 1, :], capacity) for s in range(columns)]
    for s in range(columns):
        x_ref[s * tok : (s + 1) * tok, :] = pick(one_hot_cols(slots[s][1], total), got_ref[s])
    kt_ref[...] = x_ref[:, k_cols].astype(F32).T.astype(BF16)
    vt_ref[...] = x_ref[:, v_cols].astype(F32).T.astype(BF16)
    dk_ref[...] = jnp.zeros(dk_ref.shape, F32)
    dv_ref[...] = jnp.zeros(dv_ref.shape, F32)
    joint = 2 if share % 2 == 0 else 1
    for s in range(columns):
        rows = slice(s * tok, (s + 1) * tok)
        seen = (s + 1) * tok
        place = lax.broadcasted_iota(jnp.int32, (seen, tok), 0)
        own = s * tok + lax.broadcasted_iota(jnp.int32, (seen, tok), 1)
        visible = (place >= start_ref[:, rows]) & (place <= own)
        visible = jnp.concatenate([visible.astype(F32)] * joint, axis=1) > 0.5
        for first in range(0, share, joint):
            heads = range(first, first + joint)
            q = jnp.concatenate([x_ref[rows, h * HEAD : (h + 1) * HEAD] for h in heads], axis=0)
            g = jnp.concatenate(
                [x_ref[rows, wide + h * HEAD : wide + (h + 1) * HEAD] for h in heads], axis=0
            )
            k = x_ref[:seen, k_cols]
            v = x_ref[:seen, v_cols]
            scores = lax.dot_general(k, q, across, preferred_element_type=F32)
            scores = jnp.where(visible, scores * power_scale, -jnp.inf)
            powers = jnp.exp2(scores - jnp.max(scores, axis=0, keepdims=True))
            prob = powers * (1.0 / jnp.sum(powers, axis=0, keepdims=True))
            weights = prob.astype(BF16)
            prob_grad = lax.dot_general(v, g, across, preferred_element_type=F32)
            spread = jnp.sum(prob * prob_grad, axis=0, keepdims=True)
            dscore = (prob * (prob_grad - spread) * scaling).astype(BF16)
            o_t = jnp.dot(vt_ref[:, :seen], weights, preferred_element_type=F32)
            dq_t = jnp.dot(kt_ref[:, :seen], dscore, preferred_element_type=F32)
            dk_ref[:seen, :] += jnp.dot(dscore, q, preferred_element_type=F32)
            dv_ref[:seen, :] += jnp.dot(weights, g, preferred_element_type=F32)
            for n, h in enumerate(heads):
                part = slice(n * tok, (n + 1) * tok)
                y_ref[rows, h * HEAD : (h + 1) * HEAD] = o_t[:, part].T.astype(BF16)
                y_ref[rows, wide + h * HEAD : wide + (h + 1) * HEAD] = dq_t[:, part].T.astype(BF16)
    y_ref[:, k_cols] = dk_ref[...].astype(BF16)
    y_ref[:, v_cols] = dv_ref[...].astype(BF16)
    for s in range(columns):
        out_ref[s] = pick(one_hot_rows(slots[s][0], total), y_ref[s * tok : (s + 1) * tok, :])


def params():
    return pltpu.CompilerParams(vmem_limit_bytes=VMEM_BYTES)


def pack(labels, queries, grads, keys, values, columns, total, capacity):
    tok = queries.shape[0]
    wide = queries.shape[1] // columns
    narrow = keys.shape[1] // columns
    width = 2 * (wide + narrow)

    def part(size):
        return pl.BlockSpec((tok, size), lambda c: (0, c))

    return pl.pallas_call(
        lambda *refs: pack_kernel(capacity, *refs),
        grid=(columns,),
        in_specs=[
            pl.BlockSpec((1, tok), lambda c: (0, 0)),
            part(wide),
            part(wide),
            part(narrow),
            part(narrow),
        ],
        out_specs=pl.BlockSpec((1, total, width), lambda c: (c, 0, 0)),
        out_shape=jax.ShapeDtypeStruct((columns, total, width), BF16),
        scratch_shapes=[pltpu.VMEM((total, tok), BF16)],
        compiler_params=params(),
        name="pack_rows",
    )(labels, queries, grads, keys, values)


def unpack(labels, got, wide, capacity):
    columns, total, width = got.shape
    tok = labels.shape[1]

    def part(size):
        return pl.BlockSpec((tok, size), lambda c: (0, c))

    return pl.pallas_call(
        lambda *refs: unpack_kernel(capacity, *refs),
        grid=(columns,),
        in_specs=[
            pl.BlockSpec((1, tok), lambda c: (0, 0)),
            pl.BlockSpec((1, total, width), lambda c: (c, 0, 0)),
        ],
        out_specs=[part(wide), part(wide), part(HEAD), part(HEAD)],
        out_shape=[
            jax.ShapeDtypeStruct((tok, columns * size), BF16) for size in (wide, wide, HEAD, HEAD)
        ],
        scratch_shapes=[pltpu.VMEM((tok, total), BF16)],
        compiler_params=params(),
        name="unpack_rows",
    )(labels, got)


def attend(got, sources, starts, capacity):
    columns, total, width = got.shape
    rows = starts.shape[1]
    return pl.pallas_call(
        lambda *refs: attend_kernel(capacity, *refs),
        out_shape=jax.ShapeDtypeStruct(got.shape, BF16),
        scratch_shapes=[
            pltpu.VMEM((rows, width), BF16),
            pltpu.VMEM((rows, width), BF16),
            pltpu.VMEM((HEAD, rows), BF16),
            pltpu.VMEM((HEAD, rows), BF16),
            pltpu.VMEM((rows, HEAD), F32),
            pltpu.VMEM((rows, HEAD), F32),
        ],
        compiler_params=params(),
        name="attend_group",
    )(got, sources, starts)


def swap(rows, columns, groups):
    _, total, width = rows.shape
    blocks = rows.reshape(columns * groups, total // groups, width)
    moved = lax.all_to_all(blocks, ("sp", "grp"), split_axis=0, concat_axis=0, tiled=True)
    return moved.reshape(columns, total, width)


def per_device(
    queries, key_row_matrix, value_row_matrix, out_grad, dest_group, source_group, seq_start
):
    groups = lax.axis_size("grp")
    columns = lax.axis_size("sp")
    tok = queries.shape[0]
    capacity = 2 * tok // groups
    total = groups * capacity
    wide = queries.shape[1] // columns
    with jax.named_scope("pack"):
        sent = pack(
            dest_group, queries, out_grad, key_row_matrix, value_row_matrix, columns, total, capacity
        )
    with jax.named_scope("tables"):
        sources = lax.all_gather(source_group, "sp", axis=0, tiled=True)
    with jax.named_scope("to_groups"):
        got = swap(sent, columns, groups)
    with jax.named_scope("attend"):
        done = attend(got, sources, seq_start, capacity)
    with jax.named_scope("to_homes"):
        back = swap(done, columns, groups)
    with jax.named_scope("unpack"):
        return tuple(unpack(dest_group, back, wide, capacity))


def solution(mesh):
    rows = P(("grp", "sp"), None)
    table = P("grp", "sp")
    return jax.shard_map(
        per_device,
        mesh=mesh,
        in_specs=(rows, rows, rows, rows, table, table, P("grp", None)),
        out_specs=(rows, rows, rows, rows),
        check_vma=False,
    )
```

```python
import math

import jax
import jax.numpy as jnp
from jax import lax
from jax.experimental import pallas as pl
from jax.experimental.pallas import tpu as pltpu
from jax.sharding import PartitionSpec as P

HEAD = 128
F32 = jnp.float32
BF16 = jnp.bfloat16
VMEM_BYTES = 56 * 1024 * 1024


def slot_tables(labels, capacity):
    count = labels.shape[1]
    across = jnp.broadcast_to(labels.astype(F32), (count, count))
    down = across.T
    i = lax.broadcasted_iota(jnp.int32, (count, count), 0)
    j = lax.broadcasted_iota(jnp.int32, (count, count), 1)
    same = across == down
    rank_row = jnp.sum(jnp.where(same & (i < j), 1.0, 0.0), axis=0, keepdims=True)
    rank_col = jnp.sum(jnp.where(same & (j < i), 1.0, 0.0), axis=1, keepdims=True)
    slot_row = across[:1, :] * capacity + rank_row
    slot_col = down[:, :1] * capacity + rank_col
    return slot_row.astype(jnp.int32), slot_col.astype(jnp.int32)


def one_hot_rows(slot_row, total):
    t = lax.broadcasted_iota(jnp.int32, (total, slot_row.shape[1]), 0)
    return jnp.where(t == slot_row, 1.0, 0.0).astype(BF16)


def one_hot_cols(slot_col, total):
    t = lax.broadcasted_iota(jnp.int32, (slot_col.shape[0], total), 1)
    return jnp.where(t == slot_col, 1.0, 0.0).astype(BF16)


def pick(marks, rows):
    return jnp.dot(marks, rows, preferred_element_type=F32).astype(BF16)


def pack_kernel(
    capacity, labels_ref, q_hbm, g_hbm, k_hbm, v_hbm, out_hbm, q_ref, g_ref, k_ref, v_ref, out_ref, in_sem, out_sem
):
    columns, total, _ = out_ref.shape
    wide = q_ref.shape[1] // columns
    narrow = k_ref.shape[1] // columns

    def column(c):
        pairs = ((q_hbm, q_ref, wide), (g_hbm, g_ref, wide), (k_hbm, k_ref, narrow), (v_hbm, v_ref, narrow))
        return [
            pltpu.make_async_copy(
                src.at[:, pl.ds(c * size, size)], dst.at[:, pl.ds(c * size, size)], in_sem.at[n, c]
            )
            for n, (src, dst, size) in enumerate(pairs)
        ]

    def leave(c):
        return pltpu.make_async_copy(out_ref.at[c], out_hbm.at[c], out_sem.at[c])

    for c in range(columns):
        for copy in column(c):
            copy.start()
    slot_row, _ = slot_tables(labels_ref[...], capacity)
    marks = one_hot_rows(slot_row, total)
    for c in range(columns):
        for copy in column(c):
            copy.wait()
        w = slice(c * wide, (c + 1) * wide)
        n = slice(c * narrow, (c + 1) * narrow)
        out_ref[c, :, :wide] = pick(marks, q_ref[:, w])
        out_ref[c, :, wide : 2 * wide] = pick(marks, g_ref[:, w])
        out_ref[c, :, 2 * wide :] = pick(marks, jnp.concatenate([k_ref[:, n], v_ref[:, n]], axis=1))
        leave(c).start()
    for c in range(columns):
        leave(c).wait()


def unpack_kernel(
    capacity, labels_ref, got_hbm, o_hbm, dq_hbm, dk_hbm, dv_hbm, got_ref, o_ref, dq_ref, dk_ref, dv_ref, in_sem, out_sem
):
    columns, total, _ = got_ref.shape
    wide = o_ref.shape[1] // columns
    narrow = dk_ref.shape[1] // columns

    def arrive(c):
        return pltpu.make_async_copy(got_hbm.at[c], got_ref.at[c], in_sem.at[c])

    def column(c):
        pairs = ((o_ref, o_hbm, wide), (dq_ref, dq_hbm, wide), (dk_ref, dk_hbm, narrow), (dv_ref, dv_hbm, narrow))
        return [
            pltpu.make_async_copy(
                src.at[:, pl.ds(c * size, size)], dst.at[:, pl.ds(c * size, size)], out_sem.at[n, c]
            )
            for n, (src, dst, size) in enumerate(pairs)
        ]

    for c in range(columns):
        arrive(c).start()
    _, slot_col = slot_tables(labels_ref[...], capacity)
    marks = one_hot_cols(slot_col, total)
    for c in range(columns):
        arrive(c).wait()
        w = slice(c * wide, (c + 1) * wide)
        n = slice(c * narrow, (c + 1) * narrow)
        o_ref[:, w] = pick(marks, got_ref[c, :, :wide])
        dq_ref[:, w] = pick(marks, got_ref[c, :, wide : 2 * wide])
        rest = pick(marks, got_ref[c, :, 2 * wide :])
        dk_ref[:, n] = rest[:, :narrow]
        dv_ref[:, n] = rest[:, narrow:]
        for copy in column(c):
            copy.start()
    for c in range(columns):
        for copy in column(c):
            copy.wait()


def attend_kernel(
    capacity, source_ref, start_ref, got_hbm, out_hbm, got_ref, out_ref, x_ref, s_ref, p_ref, pg_ref, w_ref, ds_ref,
    kt_ref, vt_ref, dk_ref, dv_ref, in_sem, out_sem, last_sem,
):
    columns, total, width = got_ref.shape
    tok = source_ref.shape[1]
    share = (width - 2 * HEAD) // (2 * HEAD)
    wide = share * HEAD
    scaling = 1.0 / math.sqrt(HEAD)
    power_scale = scaling * math.log2(math.e)
    across = (((1,), (1,)), ((), ()))
    k_cols = slice(2 * wide, 2 * wide + HEAD)
    v_cols = slice(2 * wide + HEAD, 2 * wide + 2 * HEAD)
    joint = 2
    lanes = joint * tok

    def arrive(s):
        return pltpu.make_async_copy(got_hbm.at[s], got_ref.at[s], in_sem.at[s])

    def leave(s):
        cols = pl.ds(0, 2 * wide)
        return pltpu.make_async_copy(out_ref.at[s, :, cols], out_hbm.at[s, :, cols], out_sem.at[s])

    def leave_last(s):
        cols = pl.ds(2 * wide, 2 * HEAD)
        return pltpu.make_async_copy(out_ref.at[s, :, cols], out_hbm.at[s, :, cols], last_sem.at[s])

    def fold(values, op):
        return op(values.reshape(tok // 8, 8, lanes), axis=0)

    for s in range(columns):
        arrive(s).start()
    slots = [slot_tables(source_ref[s : s + 1, :], capacity) for s in range(columns)]
    place = lax.broadcasted_iota(jnp.int32, (tok, lanes), 0)
    lane = lax.broadcasted_iota(jnp.int32, (tok, lanes), 1) % tok
    for s in range(columns):
        rows = slice(s * tok, (s + 1) * tok)
        seen = (s + 1) * tok
        arrive(s).wait()
        x_ref[rows, :] = pick(one_hot_cols(slots[s][1], total), got_ref[s])
        kt_ref[:, rows] = x_ref[rows, k_cols].astype(F32).T.astype(BF16)
        vt_ref[:, rows] = x_ref[rows, v_cols].astype(F32).T.astype(BF16)
        start = jnp.concatenate([start_ref[:, rows]] * joint, axis=1)
        for first in range(0, share, joint):
            heads = range(first, first + joint)
            part = slice(first * tok, first * tok + lanes)
            q = jnp.concatenate([x_ref[rows, h * HEAD : (h + 1) * HEAD] for h in heads], axis=0)
            g = jnp.concatenate(
                [x_ref[rows, wide + h * HEAD : wide + (h + 1) * HEAD] for h in heads], axis=0
            )
            top = None
            for t in range(s + 1):
                keys = slice(t * tok, (t + 1) * tok)
                scores = lax.dot_general(x_ref[keys, k_cols], q, across, preferred_element_type=F32)
                visible = place >= start - t * tok
                if t == s:
                    visible = visible & (place <= lane)
                scores = jnp.where(visible, scores, -jnp.inf)
                s_ref[keys, :] = scores
                best = fold(scores, jnp.max)
                top = best if top is None else jnp.maximum(top, best)
            top = jnp.max(top, axis=0, keepdims=True)
            mass = jnp.zeros((8, lanes), F32)
            spread = jnp.zeros((8, lanes), F32)
            for t in range(s + 1):
                keys = slice(t * tok, (t + 1) * tok)
                powers = jnp.exp2((s_ref[keys, :] - top) * power_scale)
                prob_grad = lax.dot_general(x_ref[keys, v_cols], g, across, preferred_element_type=F32)
                p_ref[keys, :] = powers
                pg_ref[keys, :] = prob_grad
                mass = mass + fold(powers, jnp.sum)
                spread = spread + fold(powers * prob_grad, jnp.sum)
            inverse = 1.0 / jnp.sum(mass, axis=0, keepdims=True)
            spread = jnp.sum(spread, axis=0, keepdims=True) * inverse
            scaled = inverse * scaling
            for t in range(s + 1):
                keys = slice(t * tok, (t + 1) * tok)
                powers = p_ref[keys, :]
                w_ref[keys, part] = (powers * inverse).astype(BF16)
                ds_ref[keys, part] = ((powers * scaled) * (pg_ref[keys, :] - spread)).astype(BF16)
        weights = w_ref[:seen, :]
        dscore = ds_ref[:seen, :]
        q = jnp.concatenate([x_ref[rows, h * HEAD : (h + 1) * HEAD] for h in range(share)], axis=0)
        g = jnp.concatenate(
            [x_ref[rows, wide + h * HEAD : wide + (h + 1) * HEAD] for h in range(share)], axis=0
        )
        marks = one_hot_rows(slots[s][0], total)
        for base, turned, pairs in ((0, vt_ref, weights), (wide, kt_ref, dscore)):
            result = jnp.dot(turned[:, :seen], pairs, preferred_element_type=F32).astype(BF16)
            stacked = jnp.concatenate([result[:, h * tok : (h + 1) * tok] for h in range(share)], axis=0)
            out_ref[s, :, base : base + wide] = lax.dot_general(
                marks, stacked, across, preferred_element_type=F32
            ).astype(BF16)
        leave(s).start()
        for total_ref, pairs, others in ((dk_ref, dscore, q), (dv_ref, weights, g)):
            result = jnp.dot(pairs, others, preferred_element_type=F32)
            if s:
                total_ref[: s * tok, :] += result[: s * tok]
            total_ref[rows, :] = result[s * tok :]
    for s in range(columns):
        rows = slice(s * tok, (s + 1) * tok)
        last = jnp.concatenate([dk_ref[rows, :], dv_ref[rows, :]], axis=1).astype(BF16)
        out_ref[s, :, 2 * wide :] = pick(one_hot_rows(slots[s][0], total), last)
        leave_last(s).start()
    for s in range(columns):
        leave(s).wait()
        leave_last(s).wait()


def params():
    return pltpu.CompilerParams(vmem_limit_bytes=VMEM_BYTES)


def pack(labels, queries, grads, keys, values, columns, total, capacity):
    width = 2 * (queries.shape[1] + keys.shape[1]) // columns
    far = pl.BlockSpec(memory_space=pl.ANY)
    return pl.pallas_call(
        lambda *refs: pack_kernel(capacity, *refs),
        in_specs=[pl.BlockSpec(memory_space=pltpu.VMEM), far, far, far, far],
        out_specs=far,
        out_shape=jax.ShapeDtypeStruct((columns, total, width), BF16),
        scratch_shapes=[
            pltpu.VMEM(queries.shape, BF16),
            pltpu.VMEM(grads.shape, BF16),
            pltpu.VMEM(keys.shape, BF16),
            pltpu.VMEM(values.shape, BF16),
            pltpu.VMEM((columns, total, width), BF16),
            pltpu.SemaphoreType.DMA((4, columns)),
            pltpu.SemaphoreType.DMA((columns,)),
        ],
        compiler_params=params(),
        name="pack_rows",
    )(labels, queries, grads, keys, values)


def unpack(labels, got, wide, capacity):
    columns, _, _ = got.shape
    tok = labels.shape[1]
    far = pl.BlockSpec(memory_space=pl.ANY)
    shapes = [(tok, columns * size) for size in (wide, wide, HEAD, HEAD)]
    return pl.pallas_call(
        lambda *refs: unpack_kernel(capacity, *refs),
        in_specs=[pl.BlockSpec(memory_space=pltpu.VMEM), far],
        out_specs=[far] * 4,
        out_shape=[jax.ShapeDtypeStruct(shape, BF16) for shape in shapes],
        scratch_shapes=[
            pltpu.VMEM(got.shape, BF16),
            *[pltpu.VMEM(shape, BF16) for shape in shapes],
            pltpu.SemaphoreType.DMA((columns,)),
            pltpu.SemaphoreType.DMA((4, columns)),
        ],
        compiler_params=params(),
        name="unpack_rows",
    )(labels, got)


def attend(got, sources, starts, capacity):
    columns, total, width = got.shape
    tok = sources.shape[1]
    rows = starts.shape[1]
    pairs = (width - 2 * HEAD) // (2 * HEAD) * tok
    near = pl.BlockSpec(memory_space=pltpu.VMEM)
    far = pl.BlockSpec(memory_space=pl.ANY)
    return pl.pallas_call(
        lambda *refs: attend_kernel(capacity, *refs),
        in_specs=[near, near, far],
        out_specs=far,
        out_shape=jax.ShapeDtypeStruct(got.shape, BF16),
        scratch_shapes=[
            pltpu.VMEM(got.shape, BF16),
            pltpu.VMEM(got.shape, BF16),
            pltpu.VMEM((rows, width), BF16),
            pltpu.VMEM((rows, 2 * tok), F32),
            pltpu.VMEM((rows, 2 * tok), F32),
            pltpu.VMEM((rows, 2 * tok), F32),
            pltpu.VMEM((rows, pairs), BF16),
            pltpu.VMEM((rows, pairs), BF16),
            pltpu.VMEM((HEAD, rows), BF16),
            pltpu.VMEM((HEAD, rows), BF16),
            pltpu.VMEM((rows, HEAD), F32),
            pltpu.VMEM((rows, HEAD), F32),
            pltpu.SemaphoreType.DMA((columns,)),
            pltpu.SemaphoreType.DMA((columns,)),
            pltpu.SemaphoreType.DMA((columns,)),
        ],
        compiler_params=params(),
        name="attend_group",
    )(sources, starts, got)


def swap(rows, columns, groups):
    _, total, width = rows.shape
    blocks = rows.reshape(columns * groups, total // groups, width)
    moved = lax.all_to_all(blocks, ("sp", "grp"), split_axis=0, concat_axis=0, tiled=True)
    return moved.reshape(columns, total, width)


def per_device(
    queries, key_row_matrix, value_row_matrix, out_grad, dest_group, source_group, seq_start
):
    groups = lax.axis_size("grp")
    columns = lax.axis_size("sp")
    tok = queries.shape[0]
    capacity = 2 * tok // groups
    total = groups * capacity
    wide = queries.shape[1] // columns
    with jax.named_scope("pack"):
        sent = pack(
            dest_group, queries, out_grad, key_row_matrix, value_row_matrix, columns, total, capacity
        )
    with jax.named_scope("tables"):
        sources = lax.all_gather(source_group, "sp", axis=0, tiled=True)
    with jax.named_scope("to_groups"):
        got = swap(sent, columns, groups)
    with jax.named_scope("attend"):
        done = attend(got, sources, seq_start, capacity)
    with jax.named_scope("to_homes"):
        back = swap(done, columns, groups)
    with jax.named_scope("unpack"):
        return tuple(unpack(dest_group, back, wide, capacity))


def solution(mesh):
    rows = P(("grp", "sp"), None)
    table = P("grp", "sp")
    return jax.shard_map(
        per_device,
        mesh=mesh,
        in_specs=(rows, rows, rows, rows, table, table, P("grp", None)),
        out_specs=(rows, rows, rows, rows),
        check_vma=False,
    )
```

```python
import math

import jax
import jax.numpy as jnp
from jax import lax
from jax.experimental import pallas as pl
from jax.experimental.pallas import tpu as pltpu
from jax.sharding import PartitionSpec as P

HEAD = 128
F32 = jnp.float32
BF16 = jnp.bfloat16
VMEM_BYTES = 28 * 1024 * 1024
PACK_VMEM_BYTES = 56 * 1024 * 1024


def slot_tables(labels, capacity):
    count = labels.shape[1]
    across = jnp.broadcast_to(labels.astype(F32), (count, count))
    down = across.T
    i = lax.broadcasted_iota(jnp.int32, (count, count), 0)
    j = lax.broadcasted_iota(jnp.int32, (count, count), 1)
    same = across == down
    rank_row = jnp.sum(jnp.where(same & (i < j), 1.0, 0.0), axis=0, keepdims=True)
    rank_col = jnp.sum(jnp.where(same & (j < i), 1.0, 0.0), axis=1, keepdims=True)
    slot_row = across[:1, :] * capacity + rank_row
    slot_col = down[:, :1] * capacity + rank_col
    return slot_row.astype(jnp.int32), slot_col.astype(jnp.int32)


def one_hot_rows(slot_row, total):
    t = lax.broadcasted_iota(jnp.int32, (total, slot_row.shape[1]), 0)
    return jnp.where(t == slot_row, 1.0, 0.0).astype(BF16)


def one_hot_cols(slot_col, total):
    t = lax.broadcasted_iota(jnp.int32, (slot_col.shape[0], total), 1)
    return jnp.where(t == slot_col, 1.0, 0.0).astype(BF16)


def pick(marks, rows):
    return jnp.dot(marks, rows, preferred_element_type=F32).astype(BF16)


def pack_kernel(
    capacity, labels_ref, q_hbm, g_hbm, k_hbm, v_hbm, out_hbm, q_ref, g_ref, k_ref, v_ref, out_ref, in_sem, out_sem
):
    columns, total, _ = out_ref.shape
    wide = q_ref.shape[1] // columns
    narrow = k_ref.shape[1] // columns

    def column(c):
        pairs = ((q_hbm, q_ref, wide), (g_hbm, g_ref, wide), (k_hbm, k_ref, narrow), (v_hbm, v_ref, narrow))
        return [
            pltpu.make_async_copy(
                src.at[:, pl.ds(c * size, size)], dst.at[:, pl.ds(c * size, size)], in_sem.at[n, c]
            )
            for n, (src, dst, size) in enumerate(pairs)
        ]

    def leave(c):
        return pltpu.make_async_copy(out_ref.at[c], out_hbm.at[c], out_sem.at[c])

    for c in range(columns):
        for copy in column(c):
            copy.start()
    slot_row, _ = slot_tables(labels_ref[...], capacity)
    marks = one_hot_rows(slot_row, total)
    for c in range(columns):
        for copy in column(c):
            copy.wait()
        w = slice(c * wide, (c + 1) * wide)
        n = slice(c * narrow, (c + 1) * narrow)
        out_ref[c, :, :wide] = pick(marks, q_ref[:, w])
        out_ref[c, :, wide : 2 * wide] = pick(marks, g_ref[:, w])
        out_ref[c, :, 2 * wide :] = pick(marks, jnp.concatenate([k_ref[:, n], v_ref[:, n]], axis=1))
        leave(c).start()
    for c in range(columns):
        leave(c).wait()


def unpack_kernel(
    capacity, labels_ref, got_ref, o_hbm, dq_hbm, dk_hbm, dv_hbm, o_ref, dq_ref, dk_ref, dv_ref, out_sem
):
    columns, total, _ = got_ref.shape
    wide = o_ref.shape[1] // columns
    narrow = dk_ref.shape[1] // columns

    def column(c):
        pairs = ((o_ref, o_hbm, wide), (dq_ref, dq_hbm, wide), (dk_ref, dk_hbm, narrow), (dv_ref, dv_hbm, narrow))
        return [
            pltpu.make_async_copy(
                src.at[:, pl.ds(c * size, size)], dst.at[:, pl.ds(c * size, size)], out_sem.at[n, c]
            )
            for n, (src, dst, size) in enumerate(pairs)
        ]

    _, slot_col = slot_tables(labels_ref[...], capacity)
    marks = one_hot_cols(slot_col, total)
    for c in range(columns):
        w = slice(c * wide, (c + 1) * wide)
        n = slice(c * narrow, (c + 1) * narrow)
        o_ref[:, w] = pick(marks, got_ref[c, :, :wide])
        dq_ref[:, w] = pick(marks, got_ref[c, :, wide : 2 * wide])
        rest = pick(marks, got_ref[c, :, 2 * wide :])
        dk_ref[:, n] = rest[:, :narrow]
        dv_ref[:, n] = rest[:, narrow:]
        for copy in column(c):
            copy.start()
    for c in range(columns):
        for copy in column(c):
            copy.wait()


def attend_kernel(
    capacity, source_ref, start_ref, got_ref, out_ref, x_ref, s_ref, p_ref, pg_ref, w_ref, ds_ref,
    kt_ref, vt_ref, dk_ref, dv_ref,
):
    columns, total, width = got_ref.shape
    tok = source_ref.shape[1]
    share = (width - 2 * HEAD) // (2 * HEAD)
    wide = share * HEAD
    scaling = 1.0 / math.sqrt(HEAD)
    power_scale = scaling * math.log2(math.e)
    across = (((1,), (1,)), ((), ()))
    k_cols = slice(2 * wide, 2 * wide + HEAD)
    v_cols = slice(2 * wide + HEAD, 2 * wide + 2 * HEAD)
    joint = 2
    lanes = joint * tok

    def fold(values, op):
        return op(values.reshape(tok // 8, 8, lanes), axis=0)

    slots = [slot_tables(source_ref[s : s + 1, :], capacity) for s in range(columns)]
    place = lax.broadcasted_iota(jnp.int32, (tok, lanes), 0)
    lane = lax.broadcasted_iota(jnp.int32, (tok, lanes), 1) % tok
    for s in range(columns):
        rows = slice(s * tok, (s + 1) * tok)
        seen = (s + 1) * tok
        x_ref[rows, :] = pick(one_hot_cols(slots[s][1], total), got_ref[s])
        kt_ref[:, rows] = x_ref[rows, k_cols].astype(F32).T.astype(BF16)
        vt_ref[:, rows] = x_ref[rows, v_cols].astype(F32).T.astype(BF16)
        start = jnp.concatenate([start_ref[:, rows]] * joint, axis=1)
        for first in range(0, share, joint):
            heads = range(first, first + joint)
            part = slice(first * tok, first * tok + lanes)
            q = jnp.concatenate([x_ref[rows, h * HEAD : (h + 1) * HEAD] for h in heads], axis=0)
            g = jnp.concatenate(
                [x_ref[rows, wide + h * HEAD : wide + (h + 1) * HEAD] for h in heads], axis=0
            )
            top = None
            for t in range(s + 1):
                keys = slice(t * tok, (t + 1) * tok)
                scores = lax.dot_general(x_ref[keys, k_cols], q, across, preferred_element_type=F32)
                visible = place >= start - t * tok
                if t == s:
                    visible = visible & (place <= lane)
                scores = jnp.where(visible, scores, -jnp.inf)
                s_ref[keys, :] = scores
                best = fold(scores, jnp.max)
                top = best if top is None else jnp.maximum(top, best)
            top = jnp.max(top, axis=0, keepdims=True)
            mass = jnp.zeros((8, lanes), F32)
            spread = jnp.zeros((8, lanes), F32)
            for t in range(s + 1):
                keys = slice(t * tok, (t + 1) * tok)
                powers = jnp.exp2((s_ref[keys, :] - top) * power_scale)
                prob_grad = lax.dot_general(x_ref[keys, v_cols], g, across, preferred_element_type=F32)
                p_ref[keys, :] = powers
                pg_ref[keys, :] = prob_grad
                mass = mass + fold(powers, jnp.sum)
                spread = spread + fold(powers * prob_grad, jnp.sum)
            inverse = 1.0 / jnp.sum(mass, axis=0, keepdims=True)
            spread = jnp.sum(spread, axis=0, keepdims=True) * inverse
            scaled = inverse * scaling
            for t in range(s + 1):
                keys = slice(t * tok, (t + 1) * tok)
                powers = p_ref[keys, :]
                w_ref[keys, part] = (powers * inverse).astype(BF16)
                ds_ref[keys, part] = ((powers * scaled) * (pg_ref[keys, :] - spread)).astype(BF16)
        weights = w_ref[:seen, :]
        dscore = ds_ref[:seen, :]
        q = jnp.concatenate([x_ref[rows, h * HEAD : (h + 1) * HEAD] for h in range(share)], axis=0)
        g = jnp.concatenate(
            [x_ref[rows, wide + h * HEAD : wide + (h + 1) * HEAD] for h in range(share)], axis=0
        )
        marks = one_hot_rows(slots[s][0], total)
        for base, turned, pairs in ((0, vt_ref, weights), (wide, kt_ref, dscore)):
            result = jnp.dot(turned[:, :seen], pairs, preferred_element_type=F32).astype(BF16)
            stacked = jnp.concatenate([result[:, h * tok : (h + 1) * tok] for h in range(share)], axis=0)
            out_ref[s, :, base : base + wide] = lax.dot_general(
                marks, stacked, across, preferred_element_type=F32
            ).astype(BF16)
        for total_ref, pairs, others in ((dk_ref, dscore, q), (dv_ref, weights, g)):
            result = jnp.dot(pairs, others, preferred_element_type=F32)
            if s:
                total_ref[: s * tok, :] += result[: s * tok]
            total_ref[rows, :] = result[s * tok :]
    for s in range(columns):
        rows = slice(s * tok, (s + 1) * tok)
        last = jnp.concatenate([dk_ref[rows, :], dv_ref[rows, :]], axis=1).astype(BF16)
        out_ref[s, :, 2 * wide :] = pick(one_hot_rows(slots[s][0], total), last)


def params(limit=VMEM_BYTES):
    return pltpu.CompilerParams(vmem_limit_bytes=limit)


def pack(labels, queries, grads, keys, values, columns, total, capacity):
    width = 2 * (queries.shape[1] + keys.shape[1]) // columns
    far = pl.BlockSpec(memory_space=pl.ANY)
    return pl.pallas_call(
        lambda *refs: pack_kernel(capacity, *refs),
        in_specs=[pl.BlockSpec(memory_space=pltpu.VMEM), far, far, far, far],
        out_specs=far,
        out_shape=jax.ShapeDtypeStruct((columns, total, width), BF16),
        scratch_shapes=[
            pltpu.VMEM(queries.shape, BF16),
            pltpu.VMEM(grads.shape, BF16),
            pltpu.VMEM(keys.shape, BF16),
            pltpu.VMEM(values.shape, BF16),
            pltpu.VMEM((columns, total, width), BF16),
            pltpu.SemaphoreType.DMA((4, columns)),
            pltpu.SemaphoreType.DMA((columns,)),
        ],
        compiler_params=params(PACK_VMEM_BYTES),
        name="pack_rows",
    )(labels, queries, grads, keys, values)


def unpack(labels, got, wide, capacity):
    columns, _, _ = got.shape
    tok = labels.shape[1]
    far = pl.BlockSpec(memory_space=pl.ANY)
    near = pl.BlockSpec(memory_space=pltpu.VMEM)
    shapes = [(tok, columns * size) for size in (wide, wide, HEAD, HEAD)]
    return pl.pallas_call(
        lambda *refs: unpack_kernel(capacity, *refs),
        in_specs=[near, near],
        out_specs=[far] * 4,
        out_shape=[jax.ShapeDtypeStruct(shape, BF16) for shape in shapes],
        scratch_shapes=[
            *[pltpu.VMEM(shape, BF16) for shape in shapes],
            pltpu.SemaphoreType.DMA((4, columns)),
        ],
        compiler_params=params(),
        name="unpack_rows",
    )(labels, got)


def attend(got, sources, starts, capacity):
    columns, total, width = got.shape
    tok = sources.shape[1]
    rows = starts.shape[1]
    pairs = (width - 2 * HEAD) // (2 * HEAD) * tok
    near = pl.BlockSpec(memory_space=pltpu.VMEM)
    return pl.pallas_call(
        lambda *refs: attend_kernel(capacity, *refs),
        in_specs=[near, near, near],
        out_specs=near,
        out_shape=pltpu.VMEM(got.shape, BF16),
        scratch_shapes=[
            pltpu.VMEM((rows, width), BF16),
            pltpu.VMEM((rows, 2 * tok), F32),
            pltpu.VMEM((rows, 2 * tok), F32),
            pltpu.VMEM((rows, 2 * tok), F32),
            pltpu.VMEM((rows, pairs), BF16),
            pltpu.VMEM((rows, pairs), BF16),
            pltpu.VMEM((HEAD, rows), BF16),
            pltpu.VMEM((HEAD, rows), BF16),
            pltpu.VMEM((rows, HEAD), F32),
            pltpu.VMEM((rows, HEAD), F32),
        ],
        compiler_params=params(),
        name="attend_group",
    )(sources, starts, got)


def swap(rows, columns, groups):
    _, total, width = rows.shape
    blocks = rows.reshape(columns * groups, total // groups, width)
    moved = lax.all_to_all(blocks, ("sp", "grp"), split_axis=0, concat_axis=0, tiled=True)
    moved = moved.reshape(columns, total, width)
    return pltpu.with_memory_space_constraint(moved, pltpu.VMEM)


def per_device(
    queries, key_row_matrix, value_row_matrix, out_grad, dest_group, source_group, seq_start
):
    groups = lax.axis_size("grp")
    columns = lax.axis_size("sp")
    tok = queries.shape[0]
    capacity = 2 * tok // groups
    total = groups * capacity
    wide = queries.shape[1] // columns
    with jax.named_scope("pack"):
        sent = pack(
            dest_group, queries, out_grad, key_row_matrix, value_row_matrix, columns, total, capacity
        )
    with jax.named_scope("tables"):
        sources = lax.all_gather(source_group, "sp", axis=0, tiled=True)
    with jax.named_scope("to_groups"):
        got = swap(sent, columns, groups)
    with jax.named_scope("attend"):
        done = attend(got, sources, seq_start, capacity)
    with jax.named_scope("to_homes"):
        back = swap(done, columns, groups)
    with jax.named_scope("unpack"):
        return tuple(unpack(dest_group, back, wide, capacity))


def solution(mesh):
    rows = P(("grp", "sp"), None)
    table = P("grp", "sp")
    return jax.shard_map(
        per_device,
        mesh=mesh,
        in_specs=(rows, rows, rows, rows, table, table, P("grp", None)),
        out_specs=(rows, rows, rows, rows),
        check_vma=False,
    )
```

```python
import math

import jax
import jax.numpy as jnp
from jax import lax
from jax.experimental import pallas as pl
from jax.experimental.pallas import tpu as pltpu
from jax.sharding import PartitionSpec as P

HEAD = 128
F32 = jnp.float32
BF16 = jnp.bfloat16
VMEM_BYTES = 56 * 1024 * 1024
UNPACK_VMEM_BYTES = 28 * 1024 * 1024


def slot_tables(labels, capacity):
    count = labels.shape[1]
    across = jnp.broadcast_to(labels.astype(F32), (count, count))
    down = across.T
    i = lax.broadcasted_iota(jnp.int32, (count, count), 0)
    j = lax.broadcasted_iota(jnp.int32, (count, count), 1)
    same = across == down
    rank_row = jnp.sum(jnp.where(same & (i < j), 1.0, 0.0), axis=0, keepdims=True)
    rank_col = jnp.sum(jnp.where(same & (j < i), 1.0, 0.0), axis=1, keepdims=True)
    slot_row = across[:1, :] * capacity + rank_row
    slot_col = down[:, :1] * capacity + rank_col
    return slot_row.astype(jnp.int32), slot_col.astype(jnp.int32)


def one_hot_rows(slot_row, total):
    t = lax.broadcasted_iota(jnp.int32, (total, slot_row.shape[1]), 0)
    return jnp.where(t == slot_row, 1.0, 0.0).astype(BF16)


def one_hot_cols(slot_col, total):
    t = lax.broadcasted_iota(jnp.int32, (slot_col.shape[0], total), 1)
    return jnp.where(t == slot_col, 1.0, 0.0).astype(BF16)


def pick(marks, rows):
    return jnp.dot(marks, rows, preferred_element_type=F32).astype(BF16)


def pack_kernel(
    capacity, labels_ref, q_hbm, g_hbm, k_hbm, v_hbm, out_hbm, q_ref, g_ref, k_ref, v_ref, out_ref, in_sem, out_sem
):
    columns, total, _ = out_ref.shape
    wide = q_ref.shape[1] // columns
    narrow = k_ref.shape[1] // columns

    parts = 2
    span = columns // parts

    def column(c):
        pairs = ((q_hbm, q_ref, wide), (g_hbm, g_ref, wide), (k_hbm, k_ref, narrow), (v_hbm, v_ref, narrow))
        return [
            pltpu.make_async_copy(
                src.at[:, pl.ds(c * span * size, span * size)],
                dst.at[:, pl.ds(c * span * size, span * size)],
                in_sem.at[n, c],
            )
            for n, (src, dst, size) in enumerate(pairs)
        ]

    def leave(c):
        return pltpu.make_async_copy(out_ref.at[c], out_hbm.at[c], out_sem.at[c])

    for c in range(parts):
        for copy in column(c):
            copy.start()
    slot_row, _ = slot_tables(labels_ref[...], capacity)
    marks = one_hot_rows(slot_row, total)
    for c in range(columns):
        if c % span == 0:
            for copy in column(c // span):
                copy.wait()
        w = slice(c * wide, (c + 1) * wide)
        n = slice(c * narrow, (c + 1) * narrow)
        out_ref[c, :, :wide] = pick(marks, q_ref[:, w])
        out_ref[c, :, wide : 2 * wide] = pick(marks, g_ref[:, w])
        out_ref[c, :, 2 * wide :] = pick(marks, jnp.concatenate([k_ref[:, n], v_ref[:, n]], axis=1))
        leave(c).start()
    for c in range(columns):
        leave(c).wait()


def unpack_kernel(
    capacity, labels_ref, got_ref, o_hbm, dq_hbm, dk_hbm, dv_hbm, o_ref, dq_ref, dk_ref, dv_ref, out_sem
):
    columns, total, _ = got_ref.shape
    wide = o_ref.shape[1] // columns
    narrow = dk_ref.shape[1] // columns

    def column(c):
        pairs = ((o_ref, o_hbm, wide), (dq_ref, dq_hbm, wide), (dk_ref, dk_hbm, narrow), (dv_ref, dv_hbm, narrow))
        return [
            pltpu.make_async_copy(
                src.at[:, pl.ds(c * size, size)], dst.at[:, pl.ds(c * size, size)], out_sem.at[n, c]
            )
            for n, (src, dst, size) in enumerate(pairs)
        ]

    _, slot_col = slot_tables(labels_ref[...], capacity)
    marks = one_hot_cols(slot_col, total)
    for c in range(columns):
        w = slice(c * wide, (c + 1) * wide)
        n = slice(c * narrow, (c + 1) * narrow)
        o_ref[:, w] = pick(marks, got_ref[c, :, :wide])
        dq_ref[:, w] = pick(marks, got_ref[c, :, wide : 2 * wide])
        rest = pick(marks, got_ref[c, :, 2 * wide :])
        dk_ref[:, n] = rest[:, :narrow]
        dv_ref[:, n] = rest[:, narrow:]
        for copy in column(c):
            copy.start()
    for c in range(columns):
        for copy in column(c):
            copy.wait()


def attend_kernel(
    capacity, source_ref, start_ref, got_hbm, out_ref, got_ref, x_ref, s_ref, p_ref, pg_ref, w_ref, ds_ref,
    kt_ref, vt_ref, dk_ref, dv_ref, in_sem,
):
    columns, total, width = got_ref.shape
    tok = source_ref.shape[1]
    share = (width - 2 * HEAD) // (2 * HEAD)
    wide = share * HEAD
    scaling = 1.0 / math.sqrt(HEAD)
    power_scale = scaling * math.log2(math.e)
    across = (((1,), (1,)), ((), ()))
    k_cols = slice(2 * wide, 2 * wide + HEAD)
    v_cols = slice(2 * wide + HEAD, 2 * wide + 2 * HEAD)
    joint = 2
    lanes = joint * tok

    def arrive(s):
        return pltpu.make_async_copy(got_hbm.at[s], got_ref.at[s], in_sem.at[s])

    def fold(values, op):
        return op(values.reshape(tok // 8, 8, lanes), axis=0)

    for s in range(columns):
        arrive(s).start()
    slots = [slot_tables(source_ref[s : s + 1, :], capacity) for s in range(columns)]
    place = lax.broadcasted_iota(jnp.int32, (tok, lanes), 0)
    lane = lax.broadcasted_iota(jnp.int32, (tok, lanes), 1) % tok

    def block(s):
        return slice(s * tok, (s + 1) * tok)

    def stack(s, base, heads):
        return jnp.concatenate(
            [x_ref[block(s), base + h * HEAD : base + (h + 1) * HEAD] for h in heads], axis=0
        )

    def receive(s):
        rows = block(s)
        if s == 0:
            arrive(0).wait()
        elif s == 1:
            for n in range(1, columns):
                arrive(n).wait()
        x_ref[rows, :] = pick(one_hot_cols(slots[s][1], total), got_ref[s])
        kt_ref[:, rows] = x_ref[rows, k_cols].astype(F32).T.astype(BF16)
        vt_ref[:, rows] = x_ref[rows, v_cols].astype(F32).T.astype(BF16)

    def softmax_steps(s, first):
        heads = range(first, first + joint)
        part = slice(first * tok, first * tok + lanes)
        side = (first // joint) % 2
        turn = s % 2
        state = {}

        def score():
            q = stack(s, 0, heads)
            start = jnp.concatenate([start_ref[:, block(s)]] * joint, axis=1)
            top = None
            for t in range(s + 1):
                keys = block(t)
                scores = lax.dot_general(x_ref[keys, k_cols], q, across, preferred_element_type=F32)
                visible = place >= start - t * tok
                if t == s:
                    visible = visible & (place <= lane)
                scores = jnp.where(visible, scores, -jnp.inf)
                s_ref[side, keys, :] = scores
                best = fold(scores, jnp.max)
                top = best if top is None else jnp.maximum(top, best)
            state["top"] = jnp.max(top, axis=0, keepdims=True)

        def power():
            g = stack(s, wide, heads)
            mass = jnp.zeros((8, lanes), F32)
            spread = jnp.zeros((8, lanes), F32)
            for t in range(s + 1):
                keys = block(t)
                powers = jnp.exp2((s_ref[side, keys, :] - state["top"]) * power_scale)
                prob_grad = lax.dot_general(x_ref[keys, v_cols], g, across, preferred_element_type=F32)
                p_ref[side, keys, :] = powers
                pg_ref[side, keys, :] = prob_grad
                mass = mass + fold(powers, jnp.sum)
                spread = spread + fold(powers * prob_grad, jnp.sum)
            state["inverse"] = 1.0 / jnp.sum(mass, axis=0, keepdims=True)
            state["spread"] = jnp.sum(spread, axis=0, keepdims=True) * state["inverse"]

        def finish():
            inverse, spread = state["inverse"], state["spread"]
            scaled = inverse * scaling
            for t in range(s + 1):
                keys = block(t)
                powers = p_ref[side, keys, :]
                w_ref[turn, keys, part] = (powers * inverse).astype(BF16)
                ds_ref[turn, keys, part] = ((powers * scaled) * (pg_ref[side, keys, :] - spread)).astype(BF16)

        return [score, power, finish]

    def product_steps(s):
        seen = (s + 1) * tok
        rows = block(s)
        turn = s % 2

        def rowwise(base, turned, pairs_ref):
            marks = one_hot_rows(slots[s][0], total)
            result = jnp.dot(turned[:, :seen], pairs_ref[turn, :seen, :], preferred_element_type=F32)
            result = result.astype(BF16)
            stacked = jnp.concatenate([result[:, h * tok : (h + 1) * tok] for h in range(share)], axis=0)
            out_ref[s, :, base : base + wide] = lax.dot_general(
                marks, stacked, across, preferred_element_type=F32
            ).astype(BF16)

        def keywise(total_ref, pairs_ref, base):
            others = stack(s, base, range(share))
            result = jnp.dot(pairs_ref[turn, :seen, :], others, preferred_element_type=F32)
            if s:
                total_ref[: s * tok, :] += result[: s * tok]
            total_ref[rows, :] = result[s * tok :]

        return [
            lambda: rowwise(0, vt_ref, w_ref),
            lambda: keywise(dv_ref, w_ref, wide),
            lambda: rowwise(wide, kt_ref, ds_ref),
            lambda: keywise(dk_ref, ds_ref, 0),
        ]

    receive(0)
    waiting = []
    for s in range(columns):
        lists = [softmax_steps(s, first) for first in range(0, share, joint)]
        work = [step for group in zip(*lists) for step in group]
        if s + 1 < columns:
            waiting = waiting + [lambda n=s + 1: receive(n)]
        for n, step in enumerate(work):
            step()
            if n < len(waiting):
                waiting[n]()
        for step in waiting[len(work) :]:
            step()
        waiting = product_steps(s)
    for step in waiting:
        step()
    for s in range(columns):
        rows = block(s)
        last = jnp.concatenate([dk_ref[rows, :], dv_ref[rows, :]], axis=1).astype(BF16)
        out_ref[s, :, 2 * wide :] = pick(one_hot_rows(slots[s][0], total), last)


def params(limit=VMEM_BYTES):
    return pltpu.CompilerParams(vmem_limit_bytes=limit)


def pack(labels, queries, grads, keys, values, columns, total, capacity):
    width = 2 * (queries.shape[1] + keys.shape[1]) // columns
    far = pl.BlockSpec(memory_space=pl.ANY)
    return pl.pallas_call(
        lambda *refs: pack_kernel(capacity, *refs),
        in_specs=[pl.BlockSpec(memory_space=pltpu.VMEM), far, far, far, far],
        out_specs=far,
        out_shape=jax.ShapeDtypeStruct((columns, total, width), BF16),
        scratch_shapes=[
            pltpu.VMEM(queries.shape, BF16),
            pltpu.VMEM(grads.shape, BF16),
            pltpu.VMEM(keys.shape, BF16),
            pltpu.VMEM(values.shape, BF16),
            pltpu.VMEM((columns, total, width), BF16),
            pltpu.SemaphoreType.DMA((4, columns)),
            pltpu.SemaphoreType.DMA((columns,)),
        ],
        compiler_params=params(),
        name="pack_rows",
    )(labels, queries, grads, keys, values)


def unpack(labels, got, wide, capacity):
    columns, _, _ = got.shape
    tok = labels.shape[1]
    far = pl.BlockSpec(memory_space=pl.ANY)
    near = pl.BlockSpec(memory_space=pltpu.VMEM)
    shapes = [(tok, columns * size) for size in (wide, wide, HEAD, HEAD)]
    return pl.pallas_call(
        lambda *refs: unpack_kernel(capacity, *refs),
        in_specs=[near, near],
        out_specs=[far] * 4,
        out_shape=[jax.ShapeDtypeStruct(shape, BF16) for shape in shapes],
        scratch_shapes=[
            *[pltpu.VMEM(shape, BF16) for shape in shapes],
            pltpu.SemaphoreType.DMA((4, columns)),
        ],
        compiler_params=params(UNPACK_VMEM_BYTES),
        name="unpack_rows",
    )(labels, got)


def attend(got, sources, starts, capacity):
    columns, total, width = got.shape
    tok = sources.shape[1]
    rows = starts.shape[1]
    pairs = (width - 2 * HEAD) // (2 * HEAD) * tok
    near = pl.BlockSpec(memory_space=pltpu.VMEM)
    return pl.pallas_call(
        lambda *refs: attend_kernel(capacity, *refs),
        in_specs=[near, near, pl.BlockSpec(memory_space=pl.ANY)],
        out_specs=near,
        out_shape=pltpu.VMEM(got.shape, BF16),
        scratch_shapes=[
            pltpu.VMEM(got.shape, BF16),
            pltpu.VMEM((rows, width), BF16),
            pltpu.VMEM((2, rows, 2 * tok), F32),
            pltpu.VMEM((2, rows, 2 * tok), F32),
            pltpu.VMEM((2, rows, 2 * tok), F32),
            pltpu.VMEM((2, rows, pairs), BF16),
            pltpu.VMEM((2, rows, pairs), BF16),
            pltpu.VMEM((HEAD, rows), BF16),
            pltpu.VMEM((HEAD, rows), BF16),
            pltpu.VMEM((rows, HEAD), F32),
            pltpu.VMEM((rows, HEAD), F32),
            pltpu.SemaphoreType.DMA((columns,)),
        ],
        compiler_params=params(),
        name="attend_group",
    )(sources, starts, got)


def swap(rows, columns, groups):
    _, total, width = rows.shape
    blocks = rows.reshape(columns * groups, total // groups, width)
    moved = lax.all_to_all(blocks, ("sp", "grp"), split_axis=0, concat_axis=0, tiled=True)
    return moved.reshape(columns, total, width)


def per_device(
    queries, key_row_matrix, value_row_matrix, out_grad, dest_group, source_group, seq_start
):
    groups = lax.axis_size("grp")
    columns = lax.axis_size("sp")
    tok = queries.shape[0]
    capacity = 2 * tok // groups
    total = groups * capacity
    wide = queries.shape[1] // columns
    with jax.named_scope("pack"):
        sent = pack(
            dest_group, queries, out_grad, key_row_matrix, value_row_matrix, columns, total, capacity
        )
    with jax.named_scope("tables"):
        sources = lax.all_gather(source_group, "sp", axis=0, tiled=True)
    with jax.named_scope("to_groups"):
        got = swap(sent, columns, groups)
    with jax.named_scope("attend"):
        done = attend(got, sources, seq_start, capacity)
    with jax.named_scope("to_homes"):
        back = pltpu.with_memory_space_constraint(swap(done, columns, groups), pltpu.VMEM)
    with jax.named_scope("unpack"):
        return tuple(unpack(dest_group, back, wide, capacity))


def solution(mesh):
    rows = P(("grp", "sp"), None)
    table = P("grp", "sp")
    return jax.shard_map(
        per_device,
        mesh=mesh,
        in_specs=(rows, rows, rows, rows, table, table, P("grp", None)),
        out_specs=(rows, rows, rows, rows),
        check_vma=False,
    )
```

```python
import math

import jax
import jax.numpy as jnp
from jax import lax
from jax.experimental import pallas as pl
from jax.experimental.pallas import tpu as pltpu
from jax.sharding import PartitionSpec as P

HEAD = 128
F32 = jnp.float32
BF16 = jnp.bfloat16
CHUNK = 8
VMEM_BYTES = 56 * 1024 * 1024
UNPACK_VMEM_BYTES = 28 * 1024 * 1024


def slot_tables(labels, capacity):
    count = labels.shape[1]
    across = jnp.broadcast_to(labels.astype(F32), (count, count))
    down = across.T
    i = lax.broadcasted_iota(jnp.int32, (count, count), 0)
    j = lax.broadcasted_iota(jnp.int32, (count, count), 1)
    same = across == down
    rank_row = jnp.sum(jnp.where(same & (i < j), 1.0, 0.0), axis=0, keepdims=True)
    rank_col = jnp.sum(jnp.where(same & (j < i), 1.0, 0.0), axis=1, keepdims=True)
    slot_row = across[:1, :] * capacity + rank_row
    slot_col = down[:, :1] * capacity + rank_col
    return slot_row.astype(jnp.int32), slot_col.astype(jnp.int32)


def one_hot_rows(slot_row, total):
    t = lax.broadcasted_iota(jnp.int32, (total, slot_row.shape[1]), 0)
    return jnp.where(t == slot_row, 1.0, 0.0).astype(BF16)


def one_hot_cols(slot_col, total):
    t = lax.broadcasted_iota(jnp.int32, (slot_col.shape[0], total), 1)
    return jnp.where(t == slot_col, 1.0, 0.0).astype(BF16)


def pick(marks, rows):
    return jnp.dot(marks, rows, preferred_element_type=F32).astype(BF16)


def pack_kernel(
    capacity, labels_ref, q_hbm, g_hbm, k_hbm, v_hbm, out_hbm, q_ref, g_ref, k_ref, v_ref, out_ref, in_sem, out_sem
):
    columns, total, _ = out_ref.shape
    wide = q_ref.shape[1] // columns
    narrow = k_ref.shape[1] // columns

    parts = 2
    span = columns // parts

    def column(c):
        pairs = ((q_hbm, q_ref, wide), (g_hbm, g_ref, wide), (k_hbm, k_ref, narrow), (v_hbm, v_ref, narrow))
        return [
            pltpu.make_async_copy(
                src.at[:, pl.ds(c * span * size, span * size)],
                dst.at[:, pl.ds(c * span * size, span * size)],
                in_sem.at[n, c],
            )
            for n, (src, dst, size) in enumerate(pairs)
        ]

    def leave(c):
        return pltpu.make_async_copy(out_ref.at[c], out_hbm.at[c], out_sem.at[c])

    for c in range(parts):
        for copy in column(c):
            copy.start()
    slot_row, _ = slot_tables(labels_ref[...], capacity)
    marks = one_hot_rows(slot_row, total)
    for c in range(columns):
        if c % span == 0:
            for copy in column(c // span):
                copy.wait()
        w = slice(c * wide, (c + 1) * wide)
        n = slice(c * narrow, (c + 1) * narrow)
        out_ref[c, :, :wide] = pick(marks, q_ref[:, w])
        out_ref[c, :, wide : 2 * wide] = pick(marks, g_ref[:, w])
        out_ref[c, :, 2 * wide :] = pick(marks, jnp.concatenate([k_ref[:, n], v_ref[:, n]], axis=1))
        leave(c).start()
    for c in range(columns):
        leave(c).wait()


def unpack_kernel(
    capacity, labels_ref, got_ref, o_hbm, dq_hbm, dk_hbm, dv_hbm, o_ref, dq_ref, dk_ref, dv_ref, out_sem
):
    columns, total, _ = got_ref.shape
    wide = o_ref.shape[1] // columns
    narrow = dk_ref.shape[1] // columns

    def column(c):
        pairs = ((o_ref, o_hbm, wide), (dq_ref, dq_hbm, wide), (dk_ref, dk_hbm, narrow), (dv_ref, dv_hbm, narrow))
        return [
            pltpu.make_async_copy(
                src.at[:, pl.ds(c * size, size)], dst.at[:, pl.ds(c * size, size)], out_sem.at[n, c]
            )
            for n, (src, dst, size) in enumerate(pairs)
        ]

    _, slot_col = slot_tables(labels_ref[...], capacity)
    marks = one_hot_cols(slot_col, total)
    for c in range(columns):
        w = slice(c * wide, (c + 1) * wide)
        n = slice(c * narrow, (c + 1) * narrow)
        o_ref[:, w] = pick(marks, got_ref[c, :, :wide])
        dq_ref[:, w] = pick(marks, got_ref[c, :, wide : 2 * wide])
        rest = pick(marks, got_ref[c, :, 2 * wide :])
        dk_ref[:, n] = rest[:, :narrow]
        dv_ref[:, n] = rest[:, narrow:]
        for copy in column(c):
            copy.start()
    for c in range(columns):
        for copy in column(c):
            copy.wait()


def attend_kernel(
    capacity, source_ref, start_ref, got_hbm, out_ref, got_ref, x_ref, s_ref, p_ref, pg_ref, w_ref, ds_ref,
    kt_ref, vt_ref, dk_ref, dv_ref, in_sem,
):
    columns, total, width = got_ref.shape
    tok = source_ref.shape[1]
    share = (width - 2 * HEAD) // (2 * HEAD)
    wide = share * HEAD
    scaling = 1.0 / math.sqrt(HEAD)
    power_scale = scaling * math.log2(math.e)
    across = (((1,), (1,)), ((), ()))
    k_cols = slice(2 * wide, 2 * wide + HEAD)
    v_cols = slice(2 * wide + HEAD, 2 * wide + 2 * HEAD)
    joint = 2
    lanes = joint * tok

    def arrive(s):
        return pltpu.make_async_copy(got_hbm.at[s], got_ref.at[s], in_sem.at[s])

    def fold(values, op):
        return op(values.reshape(values.shape[0] // 8, 8, lanes), axis=0)

    def spans(s):
        return [(t, min(t + CHUNK, s + 1)) for t in range(0, s + 1, CHUNK)]

    for s in range(columns):
        arrive(s).start()
    slots = [slot_tables(source_ref[s : s + 1, :], capacity) for s in range(columns)]
    place = lax.broadcasted_iota(jnp.int32, (CHUNK * tok, lanes), 0)
    lane = lax.broadcasted_iota(jnp.int32, (CHUNK * tok, lanes), 1) % tok

    def block(s):
        return slice(s * tok, (s + 1) * tok)

    def stack(s, base, heads):
        return jnp.concatenate(
            [x_ref[block(s), base + h * HEAD : base + (h + 1) * HEAD] for h in heads], axis=0
        )

    def receive(s):
        rows = block(s)
        for n in {0: range(2), 2: range(2, columns)}.get(s, ()):
            arrive(n).wait()
        x_ref[rows, :] = pick(one_hot_cols(slots[s][1], total), got_ref[s])
        kt_ref[:, rows] = x_ref[rows, k_cols].astype(F32).T.astype(BF16)
        vt_ref[:, rows] = x_ref[rows, v_cols].astype(F32).T.astype(BF16)

    def softmax_steps(s, first):
        heads = range(first, first + joint)
        part = slice(first * tok, first * tok + lanes)
        side = (first // joint) % 2
        turn = s % 2
        state = {}

        def score():
            q = stack(s, 0, heads)
            start = jnp.concatenate([start_ref[:, block(s)]] * joint, axis=1)
            top = None
            for t, end in spans(s):
                keys = slice(t * tok, end * tok)
                scores = lax.dot_general(x_ref[keys, k_cols], q, across, preferred_element_type=F32)
                size = (end - t) * tok
                visible = place[:size] >= start - t * tok
                if end == s + 1:
                    visible = visible & (place[:size] <= lane[:size] + (s - t) * tok)
                scores = jnp.where(visible, scores, -jnp.inf)
                s_ref[side, keys, :] = scores
                best = fold(scores, jnp.max)
                top = best if top is None else jnp.maximum(top, best)
            state["top"] = jnp.max(top, axis=0, keepdims=True)

        def power():
            g = stack(s, wide, heads)
            mass = jnp.zeros((8, lanes), F32)
            spread = jnp.zeros((8, lanes), F32)
            for t, end in spans(s):
                keys = slice(t * tok, end * tok)
                powers = jnp.exp2((s_ref[side, keys, :] - state["top"]) * power_scale)
                prob_grad = lax.dot_general(x_ref[keys, v_cols], g, across, preferred_element_type=F32)
                p_ref[side, keys, :] = powers
                pg_ref[side, keys, :] = prob_grad
                mass = mass + fold(powers, jnp.sum)
                spread = spread + fold(powers * prob_grad, jnp.sum)
            state["inverse"] = 1.0 / jnp.sum(mass, axis=0, keepdims=True)
            state["spread"] = jnp.sum(spread, axis=0, keepdims=True) * state["inverse"]

        def finish():
            inverse, spread = state["inverse"], state["spread"]
            scaled = inverse * scaling
            for t, end in spans(s):
                keys = slice(t * tok, end * tok)
                powers = p_ref[side, keys, :]
                w_ref[turn, keys, part] = (powers * inverse).astype(BF16)
                ds_ref[turn, keys, part] = ((powers * scaled) * (pg_ref[side, keys, :] - spread)).astype(BF16)

        return [score, power, finish]

    def product_steps(s):
        seen = (s + 1) * tok
        rows = block(s)
        turn = s % 2

        def rowwise(base, turned, pairs_ref):
            marks = one_hot_rows(slots[s][0], total)
            result = jnp.dot(turned[:, :seen], pairs_ref[turn, :seen, :], preferred_element_type=F32)
            result = result.astype(BF16)
            stacked = jnp.concatenate([result[:, h * tok : (h + 1) * tok] for h in range(share)], axis=0)
            out_ref[s, :, base : base + wide] = lax.dot_general(
                marks, stacked, across, preferred_element_type=F32
            ).astype(BF16)

        def keywise(total_ref, pairs_ref, base):
            others = stack(s, base, range(share))
            result = jnp.dot(pairs_ref[turn, :seen, :], others, preferred_element_type=F32)
            if s:
                total_ref[: s * tok, :] += result[: s * tok]
            total_ref[rows, :] = result[s * tok :]

        return [
            lambda: rowwise(0, vt_ref, w_ref),
            lambda: keywise(dv_ref, w_ref, wide),
            lambda: rowwise(wide, kt_ref, ds_ref),
            lambda: keywise(dk_ref, ds_ref, 0),
        ]

    receive(0)
    waiting = []
    for s in range(columns):
        lists = [softmax_steps(s, first) for first in range(0, share, joint)]
        work = [step for group in zip(*lists) for step in group]
        if s + 1 < columns:
            waiting = waiting + [lambda n=s + 1: receive(n)]
        for n, step in enumerate(work):
            step()
            if n < len(waiting):
                waiting[n]()
        for step in waiting[len(work) :]:
            step()
        waiting = product_steps(s)
    for step in waiting:
        step()
    for s in range(columns):
        rows = block(s)
        last = jnp.concatenate([dk_ref[rows, :], dv_ref[rows, :]], axis=1).astype(BF16)
        out_ref[s, :, 2 * wide :] = pick(one_hot_rows(slots[s][0], total), last)


def params(limit=VMEM_BYTES):
    return pltpu.CompilerParams(vmem_limit_bytes=limit)


def pack(labels, queries, grads, keys, values, columns, total, capacity):
    width = 2 * (queries.shape[1] + keys.shape[1]) // columns
    far = pl.BlockSpec(memory_space=pl.ANY)
    return pl.pallas_call(
        lambda *refs: pack_kernel(capacity, *refs),
        in_specs=[pl.BlockSpec(memory_space=pltpu.VMEM), far, far, far, far],
        out_specs=far,
        out_shape=jax.ShapeDtypeStruct((columns, total, width), BF16),
        scratch_shapes=[
            pltpu.VMEM(queries.shape, BF16),
            pltpu.VMEM(grads.shape, BF16),
            pltpu.VMEM(keys.shape, BF16),
            pltpu.VMEM(values.shape, BF16),
            pltpu.VMEM((columns, total, width), BF16),
            pltpu.SemaphoreType.DMA((4, columns)),
            pltpu.SemaphoreType.DMA((columns,)),
        ],
        compiler_params=params(),
        name="pack_rows",
    )(labels, queries, grads, keys, values)


def unpack(labels, got, wide, capacity):
    columns, _, _ = got.shape
    tok = labels.shape[1]
    far = pl.BlockSpec(memory_space=pl.ANY)
    near = pl.BlockSpec(memory_space=pltpu.VMEM)
    shapes = [(tok, columns * size) for size in (wide, wide, HEAD, HEAD)]
    return pl.pallas_call(
        lambda *refs: unpack_kernel(capacity, *refs),
        in_specs=[near, near],
        out_specs=[far] * 4,
        out_shape=[jax.ShapeDtypeStruct(shape, BF16) for shape in shapes],
        scratch_shapes=[
            *[pltpu.VMEM(shape, BF16) for shape in shapes],
            pltpu.SemaphoreType.DMA((4, columns)),
        ],
        compiler_params=params(UNPACK_VMEM_BYTES),
        name="unpack_rows",
    )(labels, got)


def attend(got, sources, starts, capacity):
    columns, total, width = got.shape
    tok = sources.shape[1]
    rows = starts.shape[1]
    pairs = (width - 2 * HEAD) // (2 * HEAD) * tok
    near = pl.BlockSpec(memory_space=pltpu.VMEM)
    return pl.pallas_call(
        lambda *refs: attend_kernel(capacity, *refs),
        in_specs=[near, near, pl.BlockSpec(memory_space=pl.ANY)],
        out_specs=near,
        out_shape=pltpu.VMEM(got.shape, BF16),
        scratch_shapes=[
            pltpu.VMEM(got.shape, BF16),
            pltpu.VMEM((rows, width), BF16),
            pltpu.VMEM((2, rows, 2 * tok), F32),
            pltpu.VMEM((2, rows, 2 * tok), F32),
            pltpu.VMEM((2, rows, 2 * tok), F32),
            pltpu.VMEM((2, rows, pairs), BF16),
            pltpu.VMEM((2, rows, pairs), BF16),
            pltpu.VMEM((HEAD, rows), BF16),
            pltpu.VMEM((HEAD, rows), BF16),
            pltpu.VMEM((rows, HEAD), F32),
            pltpu.VMEM((rows, HEAD), F32),
            pltpu.SemaphoreType.DMA((columns,)),
        ],
        compiler_params=params(),
        name="attend_group",
    )(sources, starts, got)


def swap(rows, columns, groups):
    _, total, width = rows.shape
    blocks = rows.reshape(columns * groups, total // groups, width)
    moved = lax.all_to_all(blocks, ("sp", "grp"), split_axis=0, concat_axis=0, tiled=True)
    return moved.reshape(columns, total, width)


def per_device(
    queries, key_row_matrix, value_row_matrix, out_grad, dest_group, source_group, seq_start
):
    groups = lax.axis_size("grp")
    columns = lax.axis_size("sp")
    tok = queries.shape[0]
    capacity = 2 * tok // groups
    total = groups * capacity
    wide = queries.shape[1] // columns
    with jax.named_scope("pack"):
        sent = pack(
            dest_group, queries, out_grad, key_row_matrix, value_row_matrix, columns, total, capacity
        )
    with jax.named_scope("tables"):
        sources = lax.all_gather(source_group, "sp", axis=0, tiled=True)
    with jax.named_scope("to_groups"):
        got = swap(sent, columns, groups)
    with jax.named_scope("attend"):
        done = attend(got, sources, seq_start, capacity)
    with jax.named_scope("to_homes"):
        back = pltpu.with_memory_space_constraint(swap(done, columns, groups), pltpu.VMEM)
    with jax.named_scope("unpack"):
        return tuple(unpack(dest_group, back, wide, capacity))


def solution(mesh):
    rows = P(("grp", "sp"), None)
    table = P("grp", "sp")
    return jax.shard_map(
        per_device,
        mesh=mesh,
        in_specs=(rows, rows, rows, rows, table, table, P("grp", None)),
        out_specs=(rows, rows, rows, rows),
        check_vma=False,
    )
```

```python
import math

import jax
import jax.numpy as jnp
from jax import lax
from jax.experimental import pallas as pl
from jax.experimental.pallas import tpu as pltpu
from jax.sharding import PartitionSpec as P

HEAD = 128
F32 = jnp.float32
BF16 = jnp.bfloat16
CHUNK = 8
VMEM_BYTES = 56 * 1024 * 1024
UNPACK_VMEM_BYTES = 28 * 1024 * 1024


def slot_tables(labels, capacity):
    count = labels.shape[1]
    across = jnp.broadcast_to(labels.astype(F32), (count, count))
    down = across.T
    i = lax.broadcasted_iota(jnp.int32, (count, count), 0)
    j = lax.broadcasted_iota(jnp.int32, (count, count), 1)
    same = across == down
    rank_row = jnp.sum(jnp.where(same & (i < j), 1.0, 0.0), axis=0, keepdims=True)
    rank_col = jnp.sum(jnp.where(same & (j < i), 1.0, 0.0), axis=1, keepdims=True)
    slot_row = across[:1, :] * capacity + rank_row
    slot_col = down[:, :1] * capacity + rank_col
    return slot_row.astype(jnp.int32), slot_col.astype(jnp.int32)


def one_hot_rows(slot_row, total):
    t = lax.broadcasted_iota(jnp.int32, (total, slot_row.shape[1]), 0)
    return jnp.where(t == slot_row, 1.0, 0.0).astype(BF16)


def one_hot_cols(slot_col, total):
    t = lax.broadcasted_iota(jnp.int32, (slot_col.shape[0], total), 1)
    return jnp.where(t == slot_col, 1.0, 0.0).astype(BF16)


def pick(marks, rows):
    return jnp.dot(marks, rows, preferred_element_type=F32).astype(BF16)


def pack_kernel(
    capacity, labels_ref, q_hbm, g_hbm, k_hbm, v_hbm, out_hbm, q_ref, g_ref, k_ref, v_ref, out_ref, in_sem, out_sem
):
    columns, total, _ = out_ref.shape
    wide = q_ref.shape[1] // columns
    narrow = k_ref.shape[1] // columns

    parts = 2
    span = columns // parts

    def column(c):
        pairs = ((q_hbm, q_ref, wide), (g_hbm, g_ref, wide), (k_hbm, k_ref, narrow), (v_hbm, v_ref, narrow))
        return [
            pltpu.make_async_copy(
                src.at[:, pl.ds(c * span * size, span * size)],
                dst.at[:, pl.ds(c * span * size, span * size)],
                in_sem.at[n, c],
            )
            for n, (src, dst, size) in enumerate(pairs)
        ]

    def leave(c):
        return pltpu.make_async_copy(out_ref.at[c], out_hbm.at[c], out_sem.at[c])

    for c in range(parts):
        for copy in column(c):
            copy.start()
    slot_row, _ = slot_tables(labels_ref[...], capacity)
    marks = one_hot_rows(slot_row, total)
    for c in range(columns):
        if c % span == 0:
            for copy in column(c // span):
                copy.wait()
        w = slice(c * wide, (c + 1) * wide)
        n = slice(c * narrow, (c + 1) * narrow)
        out_ref[c, :, :wide] = pick(marks, q_ref[:, w])
        out_ref[c, :, wide : 2 * wide] = pick(marks, g_ref[:, w])
        out_ref[c, :, 2 * wide :] = pick(marks, jnp.concatenate([k_ref[:, n], v_ref[:, n]], axis=1))
        leave(c).start()
    for c in range(columns):
        leave(c).wait()


def unpack_kernel(
    marks_ref, got_ref, o_hbm, dq_hbm, dk_hbm, dv_hbm, o_ref, dq_ref, dk_ref, dv_ref, out_sem
):
    columns = got_ref.shape[0]
    wide = o_ref.shape[1] // columns
    narrow = dk_ref.shape[1] // columns

    def column(c):
        pairs = ((o_ref, o_hbm, wide), (dq_ref, dq_hbm, wide), (dk_ref, dk_hbm, narrow), (dv_ref, dv_hbm, narrow))
        return [
            pltpu.make_async_copy(
                src.at[:, pl.ds(c * size, size)], dst.at[:, pl.ds(c * size, size)], out_sem.at[n, c]
            )
            for n, (src, dst, size) in enumerate(pairs)
        ]

    marks = marks_ref[...]
    for c in range(columns):
        w = slice(c * wide, (c + 1) * wide)
        n = slice(c * narrow, (c + 1) * narrow)
        o_ref[:, w] = pick(marks, got_ref[c, :, :wide])
        dq_ref[:, w] = pick(marks, got_ref[c, :, wide : 2 * wide])
        rest = pick(marks, got_ref[c, :, 2 * wide :])
        dk_ref[:, n] = rest[:, :narrow]
        dv_ref[:, n] = rest[:, narrow:]
        for copy in column(c):
            copy.start()
    for c in range(columns):
        for copy in column(c):
            copy.wait()


def home_marks_kernel(capacity, labels_ref, marks_ref):
    _, slot_col = slot_tables(labels_ref[...], capacity)
    marks_ref[...] = one_hot_cols(slot_col, marks_ref.shape[1])


def attend_kernel(
    capacity, source_ref, start_ref, got_hbm, out_ref, got_ref, x_ref, s_ref, p_ref, pg_ref, w_ref, ds_ref,
    kt_ref, vt_ref, dk_ref, dv_ref, in_sem,
):
    columns, total, width = got_ref.shape
    tok = source_ref.shape[1]
    share = (width - 2 * HEAD) // (2 * HEAD)
    wide = share * HEAD
    scaling = 1.0 / math.sqrt(HEAD)
    power_scale = scaling * math.log2(math.e)
    across = (((1,), (1,)), ((), ()))
    k_cols = slice(2 * wide, 2 * wide + HEAD)
    v_cols = slice(2 * wide + HEAD, 2 * wide + 2 * HEAD)
    joint = 2
    lanes = joint * tok

    def arrive(s):
        return pltpu.make_async_copy(got_hbm.at[s], got_ref.at[s], in_sem.at[s])

    def fold(values, op):
        return op(values.reshape(values.shape[0] // 8, 8, lanes), axis=0)

    def spans(s):
        return [(t, min(t + CHUNK, s + 1)) for t in range(0, s + 1, CHUNK)]

    for s in range(columns):
        arrive(s).start()
    slots = [slot_tables(source_ref[s : s + 1, :], capacity) for s in range(columns)]
    place = lax.broadcasted_iota(jnp.int32, (CHUNK * tok, lanes), 0)
    lane = lax.broadcasted_iota(jnp.int32, (CHUNK * tok, lanes), 1) % tok

    def block(s):
        return slice(s * tok, (s + 1) * tok)

    def stack(s, base, heads):
        return jnp.concatenate(
            [x_ref[block(s), base + h * HEAD : base + (h + 1) * HEAD] for h in heads], axis=0
        )

    def receive(s):
        rows = block(s)
        for n in {0: range(2), 2: range(2, columns)}.get(s, ()):
            arrive(n).wait()
        x_ref[rows, :] = pick(one_hot_cols(slots[s][1], total), got_ref[s])
        kt_ref[:, rows] = x_ref[rows, k_cols].astype(F32).T.astype(BF16)
        vt_ref[:, rows] = x_ref[rows, v_cols].astype(F32).T.astype(BF16)

    def softmax_steps(s, first):
        heads = range(first, first + joint)
        part = slice(first * tok, first * tok + lanes)
        side = (first // joint) % 2
        turn = s % 2
        state = {}

        def score():
            q = stack(s, 0, heads)
            start = jnp.concatenate([start_ref[:, block(s)]] * joint, axis=1)
            top = None
            for t, end in spans(s):
                keys = slice(t * tok, end * tok)
                scores = lax.dot_general(x_ref[keys, k_cols], q, across, preferred_element_type=F32)
                size = (end - t) * tok
                visible = place[:size] >= start - t * tok
                if end == s + 1:
                    visible = visible & (place[:size] <= lane[:size] + (s - t) * tok)
                scores = jnp.where(visible, scores, -jnp.inf)
                s_ref[side, keys, :] = scores
                best = fold(scores, jnp.max)
                top = best if top is None else jnp.maximum(top, best)
            state["top"] = jnp.max(top, axis=0, keepdims=True)

        def power():
            g = stack(s, wide, heads)
            mass = jnp.zeros((8, lanes), F32)
            spread = jnp.zeros((8, lanes), F32)
            for t, end in spans(s):
                keys = slice(t * tok, end * tok)
                powers = jnp.exp2((s_ref[side, keys, :] - state["top"]) * power_scale)
                prob_grad = lax.dot_general(x_ref[keys, v_cols], g, across, preferred_element_type=F32)
                p_ref[side, keys, :] = powers
                pg_ref[side, keys, :] = prob_grad
                mass = mass + fold(powers, jnp.sum)
                spread = spread + fold(powers * prob_grad, jnp.sum)
            state["inverse"] = 1.0 / jnp.sum(mass, axis=0, keepdims=True)
            state["spread"] = jnp.sum(spread, axis=0, keepdims=True) * state["inverse"]

        def finish():
            inverse, spread = state["inverse"], state["spread"]
            scaled = inverse * scaling
            for t, end in spans(s):
                keys = slice(t * tok, end * tok)
                powers = p_ref[side, keys, :]
                w_ref[turn, keys, part] = (powers * inverse).astype(BF16)
                ds_ref[turn, keys, part] = ((powers * scaled) * (pg_ref[side, keys, :] - spread)).astype(BF16)

        return [score, power, finish]

    def product_steps(s, heads):
        part = slice(heads[0] * tok, (heads[-1] + 1) * tok)
        span = slice(heads[0] * HEAD, (heads[-1] + 1) * HEAD)
        seen = (s + 1) * tok
        rows = block(s)
        turn = s % 2

        def rowwise(base, turned, pairs_ref):
            marks = one_hot_rows(slots[s][0], total)
            result = jnp.dot(turned[:, :seen], pairs_ref[turn, :seen, part], preferred_element_type=F32)
            result = result.astype(BF16)
            stacked = jnp.concatenate([result[:, h * tok : (h + 1) * tok] for h in range(len(heads))], axis=0)
            out_ref[s, :, base + span.start : base + span.stop] = lax.dot_general(
                marks, stacked, across, preferred_element_type=F32
            ).astype(BF16)

        def keywise(total_ref, pairs_ref, base):
            others = stack(s, base, heads)
            result = jnp.dot(pairs_ref[turn, :seen, part], others, preferred_element_type=F32)
            if s:
                total_ref[: s * tok, :] += result[: s * tok]
            if heads[0]:
                total_ref[rows, :] += result[s * tok :]
            else:
                total_ref[rows, :] = result[s * tok :]

        return [
            lambda: rowwise(0, vt_ref, w_ref),
            lambda: keywise(dv_ref, w_ref, wide),
            lambda: rowwise(wide, kt_ref, ds_ref),
            lambda: keywise(dk_ref, ds_ref, 0),
        ]

    def weave(work, waiting):
        for n, step in enumerate(work):
            step()
            if n < len(waiting):
                waiting[n]()
        for step in waiting[len(work) :]:
            step()

    receive(0)
    waiting = []
    for s in range(columns):
        lists = [softmax_steps(s, first) for first in range(0, share, joint)]
        if s + 1 < columns:
            waiting = waiting + [lambda n=s + 1: receive(n)]
        if s + 1 == columns:
            for first, work in zip(range(0, share, joint), lists):
                weave(work, waiting)
                waiting = product_steps(s, range(first, first + joint))
        else:
            weave([step for group in zip(*lists) for step in group], waiting)
            waiting = product_steps(s, range(share))
    for step in waiting:
        step()
    for s in range(columns):
        rows = block(s)
        last = jnp.concatenate([dk_ref[rows, :], dv_ref[rows, :]], axis=1).astype(BF16)
        out_ref[s, :, 2 * wide :] = pick(one_hot_rows(slots[s][0], total), last)


def params(limit=VMEM_BYTES):
    return pltpu.CompilerParams(vmem_limit_bytes=limit)


def pack(labels, queries, grads, keys, values, columns, total, capacity):
    width = 2 * (queries.shape[1] + keys.shape[1]) // columns
    far = pl.BlockSpec(memory_space=pl.ANY)
    return pl.pallas_call(
        lambda *refs: pack_kernel(capacity, *refs),
        in_specs=[pl.BlockSpec(memory_space=pltpu.VMEM), far, far, far, far],
        out_specs=far,
        out_shape=jax.ShapeDtypeStruct((columns, total, width), BF16),
        scratch_shapes=[
            pltpu.VMEM(queries.shape, BF16),
            pltpu.VMEM(grads.shape, BF16),
            pltpu.VMEM(keys.shape, BF16),
            pltpu.VMEM(values.shape, BF16),
            pltpu.VMEM((columns, total, width), BF16),
            pltpu.SemaphoreType.DMA((4, columns)),
            pltpu.SemaphoreType.DMA((columns,)),
        ],
        compiler_params=params(),
        name="pack_rows",
    )(labels, queries, grads, keys, values)


def home_marks(labels, total, capacity):
    near = pl.BlockSpec(memory_space=pltpu.VMEM)
    return pl.pallas_call(
        lambda *refs: home_marks_kernel(capacity, *refs),
        in_specs=[near],
        out_specs=near,
        out_shape=jax.ShapeDtypeStruct((labels.shape[1], total), BF16),
        compiler_params=params(UNPACK_VMEM_BYTES),
        name="home_marks",
    )(labels)


def unpack(marks, got, wide):
    columns, _, _ = got.shape
    tok = marks.shape[0]
    far = pl.BlockSpec(memory_space=pl.ANY)
    near = pl.BlockSpec(memory_space=pltpu.VMEM)
    shapes = [(tok, columns * size) for size in (wide, wide, HEAD, HEAD)]
    return pl.pallas_call(
        unpack_kernel,
        in_specs=[near, near],
        out_specs=[far] * 4,
        out_shape=[jax.ShapeDtypeStruct(shape, BF16) for shape in shapes],
        scratch_shapes=[
            *[pltpu.VMEM(shape, BF16) for shape in shapes],
            pltpu.SemaphoreType.DMA((4, columns)),
        ],
        compiler_params=params(UNPACK_VMEM_BYTES),
        name="unpack_rows",
    )(marks, got)


def attend(got, sources, starts, capacity):
    columns, total, width = got.shape
    tok = sources.shape[1]
    rows = starts.shape[1]
    pairs = (width - 2 * HEAD) // (2 * HEAD) * tok
    near = pl.BlockSpec(memory_space=pltpu.VMEM)
    return pl.pallas_call(
        lambda *refs: attend_kernel(capacity, *refs),
        in_specs=[near, near, pl.BlockSpec(memory_space=pl.ANY)],
        out_specs=near,
        out_shape=pltpu.VMEM(got.shape, BF16),
        scratch_shapes=[
            pltpu.VMEM(got.shape, BF16),
            pltpu.VMEM((rows, width), BF16),
            pltpu.VMEM((2, rows, 2 * tok), F32),
            pltpu.VMEM((2, rows, 2 * tok), F32),
            pltpu.VMEM((2, rows, 2 * tok), F32),
            pltpu.VMEM((2, rows, pairs), BF16),
            pltpu.VMEM((2, rows, pairs), BF16),
            pltpu.VMEM((HEAD, rows), BF16),
            pltpu.VMEM((HEAD, rows), BF16),
            pltpu.VMEM((rows, HEAD), F32),
            pltpu.VMEM((rows, HEAD), F32),
            pltpu.SemaphoreType.DMA((columns,)),
        ],
        compiler_params=params(),
        name="attend_group",
    )(sources, starts, got)


def swap(rows, columns, groups):
    _, total, width = rows.shape
    blocks = rows.reshape(columns * groups, total // groups, width)
    moved = lax.all_to_all(blocks, ("sp", "grp"), split_axis=0, concat_axis=0, tiled=True)
    return moved.reshape(columns, total, width)


def per_device(
    queries, key_row_matrix, value_row_matrix, out_grad, dest_group, source_group, seq_start
):
    groups = lax.axis_size("grp")
    columns = lax.axis_size("sp")
    tok = queries.shape[0]
    capacity = 2 * tok // groups
    total = groups * capacity
    wide = queries.shape[1] // columns
    with jax.named_scope("pack"):
        sent = pack(
            dest_group, queries, out_grad, key_row_matrix, value_row_matrix, columns, total, capacity
        )
    with jax.named_scope("tables"):
        sources = lax.all_gather(source_group, "sp", axis=0, tiled=True)
        sources, labels = lax.optimization_barrier((sources, dest_group))
        marks = home_marks(labels, total, capacity)
    with jax.named_scope("to_groups"):
        got = swap(sent, columns, groups)
    with jax.named_scope("attend"):
        done = attend(got, sources, seq_start, capacity)
    with jax.named_scope("to_homes"):
        back = pltpu.with_memory_space_constraint(swap(done, columns, groups), pltpu.VMEM)
    with jax.named_scope("unpack"):
        return tuple(unpack(marks, back, wide))


def solution(mesh):
    rows = P(("grp", "sp"), None)
    table = P("grp", "sp")
    return jax.shard_map(
        per_device,
        mesh=mesh,
        in_specs=(rows, rows, rows, rows, table, table, P("grp", None)),
        out_specs=(rows, rows, rows, rows),
        check_vma=False,
    )
```
